32 devices in a mesh: gx: 4 (over y, core), gy: 8 (over z, x).
Axes of the slice: x: 2, y: 2, z: 4, core: 2. Of those that a mesh axis runs over, the one named last changes fastest.
Arguments:
- right_sides: float32 [16, 4, 16, 1024], P(None, None, 'gx', 'gy'), may hold values from -12 to 12, as said below
- coefficients: float32 [27, 4, 16, 1024], P(None, None, 'gx', 'gy'), may hold values from -0.045 to 2, as said below
Outputs:
- basis_q: float32 [80, 4, 16, 1024], P(None, None, 'gx', 'gy')
- factor_r: float32 [80, 80], replicated
The draws below stay inside these ranges and needn't reach their ends.
Inputs may be any that keep to these rules, and one draw needn't show every extreme that they name: `right_sides`: each entry is the product of a value of order one and a factor that grows from 1 to 3 along x. `coefficients`: the centre coefficient (index 13) lies in 1 to 2, the other 26 in -0.045 to 0.015.
All inputs are finite; a program needn't handle non-finite values.
Results may differ from the reference program's by a relative error of at most 0.0003.
Values sent between devices are 32-bit elements; how exact they have to be, the bound alone decides.
A program may use at most 64 MiB of HBM per device.

```python
import jax
import jax.numpy as jnp
from jax import lax

RHS = 16
STEPS = 4
NX = 16
NY = 1024
NZ = 4


def draw_right_sides(key, part):
    ramp = jnp.power(jnp.float32(3.0), jnp.arange(NX, dtype=jnp.float32) / jnp.float32(NX - 1))
    values = jnp.clip(jax.random.normal(key, (RHS, NZ, NX, NY), jnp.float32), -4.0, 4.0)
    return values * ramp[None, None, :, None]


def draw_coefficients(key, part):
    first = jax.random.uniform(jax.random.fold_in(key, 1), (27, NZ, NX, NY), jnp.float32)
    second = jax.random.uniform(jax.random.fold_in(key, 2), (27, NZ, NX, NY), jnp.float32)
    others = -0.03 * first + 0.015 * (2.0 * second - 1.0)
    middle = 1.0 + second[13]
    marker = (jnp.arange(27) == 13)[:, None, None, None]
    return jnp.where(marker, middle[None], others)


def setup_inputs(seed: int = 0) -> dict:
    key_of = jax.random.split(jax.random.key(seed), 3)
    right_sides = draw_right_sides(jax.random.fold_in(key_of[2], 71), 0)
    coefficients = draw_coefficients(jax.random.fold_in(key_of[2], 71), 0)
    return {"right_sides": right_sides, "coefficients": coefficients}


OFFSETS = tuple(((plane_step, row_step, col_step) for plane_step in (-1, 0, 1) for row_step in (-1, 0, 1) for col_step in (-1, 0, 1)))
CENTER_SHIFT = 1.5
HALF_SPAN = 0.5

def apply_operator(padded, coefficients):
    planes, rows, columns = (coefficients.shape[1], coefficients.shape[2], coefficients.shape[3])
    result = jnp.zeros((padded.shape[0], planes, rows, columns), jnp.float32)
    for number, (plane_step, row_step, col_step) in enumerate(OFFSETS):
        window = padded[:, 1 + plane_step:1 + plane_step + planes, 1 + row_step:1 + row_step + rows, 1 + col_step:1 + col_step + columns]
        result = result + coefficients[number][None] * window
    return result

def chebyshev_next(padded, coefficients, previous):
    center = padded[:, 1:-1, 1:-1, 1:-1]
    shifted = (apply_operator(padded, coefficients) - CENTER_SHIFT * center) / HALF_SPAN
    if previous is None:
        return shifted
    return 2.0 * shifted - previous

def pad_grid(vectors):
    wrapped = jnp.pad(vectors, ((0, 0), (0, 0), (1, 1), (0, 0)), mode='wrap')
    return jnp.pad(wrapped, ((0, 0), (1, 1), (0, 0), (1, 1)))

def reference(right_sides, coefficients):
    blocks = [right_sides]
    previous = None
    current = right_sides
    for step in range(STEPS):
        following = chebyshev_next(pad_grid(current), coefficients, previous)
        previous, current = (current, following)
        blocks.append(current)
    stacked = jnp.concatenate(blocks, axis=0)
    flat = stacked.reshape(stacked.shape[0], -1)
    gram = jnp.dot(flat, flat.T, precision=lax.Precision.HIGHEST) / jnp.float32(flat.shape[1])
    factor_lower = jnp.linalg.cholesky(gram)
    identity = jnp.eye(flat.shape[0], dtype=jnp.float32)
    inverse = jax.scipy.linalg.solve_triangular(factor_lower, identity, lower=True)
    solved = jnp.dot(inverse, flat, precision=lax.Precision.HIGHEST)
    return (solved.reshape(stacked.shape), factor_lower.T)
```

```python
import functools

import jax
import jax.numpy as jnp
from jax import lax
from jax.experimental import pallas as pl
from jax.experimental.pallas import tpu as pltpu
from jax.sharding import PartitionSpec as P

MESH = pl.DeviceIdType.MESH
STEPS = 4
BLOCKS = STEPS + 1
LANES = 128
SIDES = (0, 1)
NT = (((1,), (1,)), ((), ()))
NN = (((1,), (0,)), ((), ()))


def dot(a, b, dims):
    return lax.dot_general(
        a, b, dims, precision=lax.Precision.HIGHEST, preferred_element_type=jnp.float32
    )


def each(start, stop, body):
    if stop - start <= 8:
        for i in range(start, stop):
            body(i)
    else:
        lax.fori_loop(start, stop, lambda i, c: (body(i), c)[1], 0)


def factor(square, rhs):
    row = lax.broadcasted_iota(jnp.int32, (rhs, LANES), 0)
    lane = lax.broadcasted_iota(jnp.int32, (rhs, LANES), 1)
    work = jnp.where(lane < rhs, square, jnp.where(lane - rhs == row, 1.0, 0.0))
    lower = jnp.zeros((rhs, LANES), jnp.float32)
    scale = jnp.zeros((rhs, LANES), jnp.float32)
    for k in range(rhs):
        column = jnp.broadcast_to(work[:, k : k + 1], (rhs, LANES))
        pivot_row = jnp.broadcast_to(work[k : k + 1, :], (rhs, LANES))
        pivot = jnp.broadcast_to(column[k : k + 1, :], (rhs, LANES))
        root = 1.0 / jnp.sqrt(pivot)
        lower = jnp.where((lane == k) & (row >= k), column * root, lower)
        scale = jnp.where(row == k, root, scale)
        work = work - jnp.where(row > k, column * (1.0 / pivot), 0.0) * pivot_row
    inverse = pltpu.roll(work * scale, LANES - rhs, 1)
    return lower, jnp.where(lane <= row, inverse, 0.0)


def kernel(
    nx, ny, rhs, nz, rows, total_cells,
    v_hbm, c_hbm, q_hbm, l_ref,
    v_in, c_in, wide, basis, tile, ghost, packed, landed, shifted, gram_x, gram_y,
    lower_inv, out,
    load_sem, store_sem, halo_send, halo_recv, gx_send, gx_recv, gy_send, gy_recv,
):
    gx, gy = lax.axis_index("gx"), lax.axis_index("gy")
    cells = nz * rows
    up, down = lax.rem(gx + 1, nx), lax.rem(gx + nx - 1, nx)
    has_left, has_right = gy > 0, gy < ny - 1
    around = (down, gx, up)
    there = (gy - 1, gy + 1)
    present = (has_left, has_right)

    load_v = pltpu.make_async_copy(v_hbm, v_in, load_sem.at[0])
    load_c = pltpu.make_async_copy(c_hbm, c_in, load_sem.at[1])
    load_v.start()
    load_c.start()

    barrier = pltpu.get_barrier_semaphore()

    def greet(x, y):
        pl.semaphore_signal(barrier, inc=1, device_id={"gx": x, "gy": y}, device_id_type=MESH)

    each(1, nx, lambda i: greet(lax.rem(gx + i, nx), gy))
    each(1, ny, lambda i: greet(gx, lax.rem(gy + i, ny)))
    for side in SIDES:
        @pl.when(present[side])
        def _():
            greet(down, there[side])
            greet(up, there[side])
    corners = 2 * has_left.astype(jnp.int32) + 2 * has_right.astype(jnp.int32)
    pl.semaphore_wait(barrier, (nx - 1) + (ny - 1) + corners)

    lane = lax.broadcasted_iota(jnp.int32, (rhs, LANES), 1)

    for side in SIDES:
        @pl.when(jnp.logical_not(present[side]))
        def _():
            for s in range(STEPS):
                landed[s, side] = jnp.zeros((3, rhs, LANES), jnp.float32)

    lower_inv[...] = jnp.zeros_like(lower_inv)

    def row_copy(s, side):
        return pltpu.make_async_remote_copy(
            src_ref=tile.at[s, :, rows - 1 if side == 0 else 0],
            dst_ref=ghost.at[s, side],
            send_sem=halo_send.at[s, side],
            recv_sem=halo_recv.at[s, side],
            device_id={"gx": up if side == 0 else down, "gy": gy},
            device_id_type=MESH,
        )

    def column_copy(s, side, slot):
        return pltpu.make_async_remote_copy(
            src_ref=packed.at[s, side],
            dst_ref=landed.at[s, side, slot],
            send_sem=halo_send.at[s, 2 + 3 * side + slot],
            recv_sem=halo_recv.at[s, 2 + 3 * side + slot],
            device_id={"gx": around[2 - slot], "gy": there[1 - side]},
            device_id_type=MESH,
        )

    def send_halo(s):
        for side in SIDES:
            row_copy(s, side).start()
        right = jnp.zeros((rhs, LANES), jnp.float32)
        left = jnp.zeros((rhs, LANES), jnp.float32)
        for number in range(cells):
            value = tile[s, number // rows, number % rows]
            right = jnp.where(lane == number, pltpu.roll(value, number + 1, 1), right)
            moved = pltpu.roll(value, number, 1) if number else value
            left = jnp.where(lane == number, moved, left)
        packed[s, 0] = right
        packed[s, 1] = left
        for side in SIDES:
            @pl.when(present[1 - side])
            def _():
                for slot in range(3):
                    column_copy(s, side, slot).start()

    def wait_halo(s):
        for side in SIDES:
            row_copy(s, side).wait_recv()
        for side in SIDES:
            @pl.when(present[side])
            def _():
                for slot in range(3):
                    column_copy(s, side, slot).wait_recv()

    def finish_halo(s):
        for side in SIDES:
            row_copy(s, side).wait_send()
            @pl.when(present[1 - side])
            def _():
                for slot in range(3):
                    column_copy(s, side, slot).wait_send()

    def build_shifted(s):
        for padded in range(rows + 2):
            slot = 0 if padded == 0 else 2 if padded == rows + 1 else 1
            before, after = landed[s, 0, slot], landed[s, 1, slot]
            x = (padded - 1) % rows
            for z in range(nz):
                if slot == 1:
                    value = tile[s, z, x]
                else:
                    value = ghost[s, slot // 2, z]
                number = z * rows + x
                edge = pltpu.roll(before, LANES - 1 - number, 1)
                shifted[0, z, padded] = pltpu.roll(jnp.where(lane == LANES - 1, edge, value), 1, 1)
                shifted[1, z, padded] = value
                edge = pltpu.roll(after, LANES - number, 1) if number else after
                shifted[2, z, padded] = pltpu.roll(jnp.where(lane == 0, edge, value), LANES - 1, 1)

    def apply_operator(s):
        block = s * rhs
        for z in range(nz):
            total = jnp.zeros((rows, rhs // 8, 8, LANES), jnp.float32)
            for dz in (-1, 0, 1):
                if not 0 <= z + dz < nz:
                    continue
                for dx in (-1, 0, 1):
                    for dy in (-1, 0, 1):
                        number = 9 * (dz + 1) + 3 * (dx + 1) + (dy + 1)
                        weight = wide[number, z * rows : (z + 1) * rows]
                        window = shifted[dy + 1, z + dz, 1 + dx : 1 + dx + rows]
                        total = total + weight[:, None] * window.reshape(total.shape)
            total = total.reshape(rows, rhs, LANES)
            for x in range(rows):
                here = pl.ds((z * rows + x) * LANES, LANES)
                value = total[x]
                if s > 0:
                    value = 2.0 * value - basis[pl.ds(block - rhs, rhs), here]
                basis[pl.ds(block + rhs, rhs), here] = value
                if s + 1 < STEPS:
                    tile[s + 1, z, x] = value

    def gx_copy(j, slot, x):
        return pltpu.make_async_remote_copy(
            src_ref=gram_x.at[j, slot], dst_ref=gram_x.at[j, slot],
            send_sem=gx_send.at[j, x], recv_sem=gx_recv.at[j, slot],
            device_id={"gx": x, "gy": gy}, device_id_type=MESH,
        )

    def gy_copy(j, slot, y):
        return pltpu.make_async_remote_copy(
            src_ref=gram_y.at[j, slot], dst_ref=gram_y.at[j, slot],
            send_sem=gy_send.at[j, y], recv_sem=gy_recv.at[j, slot],
            device_id={"gx": gx, "gy": y}, device_id_type=MESH,
        )

    def local_gram(j):
        upto = (j + 1) * rhs
        part = dot(basis[j * rhs : upto, :], basis[0:upto, :], NT)
        gram_x[j, gx] = jnp.concatenate(
            [part, jnp.zeros((rhs, LANES - upto), jnp.float32)], axis=1
        )
        def go(i):
            gx_copy(j, gx, lax.rem(gx + i, nx)).start()
        each(1, nx, go)

    def gram_over_gx(j):
        def wait(i):
            other = lax.rem(gx + i, nx)
            gx_copy(j, other, other).wait_recv()
        each(1, nx, wait)
        gram_y[j, gy] = jnp.sum(gram_x[j], axis=0)
        def go(i):
            gy_copy(j, gy, lax.rem(gy + i, ny)).start()
        each(1, ny, go)

    def gram_over_gy(j):
        def wait(i):
            other = lax.rem(gy + i, ny)
            gy_copy(j, other, other).wait_recv()
        each(1, ny, wait)
        return jnp.sum(gram_y[j], axis=0) / jnp.float32(total_cells)

    def finish_gram(j):
        def done_x(i):
            gx_copy(j, gx, lax.rem(gx + i, nx)).wait_send()
        each(1, nx, done_x)
        def done_y(i):
            gy_copy(j, gy, lax.rem(gy + i, ny)).wait_send()
        each(1, ny, done_y)

    def factor_block(j):
        gram = gram_over_gy(j)
        at = j * rhs
        here = slice(at, at + rhs)
        if j == 0:
            lower, inverse = factor(gram, rhs)
            l_ref[here, :] = lower
            lower_inv[here, :] = inverse
            return
        known = lower_inv[...]
        panel = jnp.where(lane < at, dot(gram, known, NT), 0.0)
        square = pltpu.roll(gram, LANES - at, 1) - jnp.concatenate(
            [dot(panel, panel, NT), jnp.zeros((rhs, LANES - rhs), jnp.float32)], axis=1
        )
        lower, inverse = factor(square, rhs)
        l_ref[here, :] = panel + pltpu.roll(lower, at, 1)
        update = dot(dot(inverse[:, :rhs], panel, NN), known, NN)
        lower_inv[here, :] = pltpu.roll(inverse, at, 1) - update

    def store(j):
        return pltpu.make_async_copy(
            out.at[j], q_hbm.at[pl.ds(j * rhs * cells, rhs * cells), :], store_sem.at[j]
        )

    def apply_block(j):
        at = j * rhs
        upto = at + rhs
        rows_j = lower_inv[at:upto, 0:upto]
        solved = dot(rows_j, basis[0:upto, :], NN)
        for number in range(cells):
            out[j, pl.ds(number, rhs, stride=cells), :] = solved[
                :, number * LANES : (number + 1) * LANES
            ]
        store(j).start()

    load_v.wait()
    for number in range(cells):
        value = v_in[pl.ds(number, rhs, stride=cells), :]
        tile[0, number // rows, number % rows] = value
        basis[0:rhs, number * LANES : (number + 1) * LANES] = value

    for s in range(STEPS):
        send_halo(s)
        if s == 0:
            load_c.wait()
            def widen(number, carry):
                values = c_in[pl.ds(number * cells, cells), :]
                center = jnp.where(number == 13, 3.0, 0.0)
                wide[number] = jnp.broadcast_to(
                    (2.0 * values - center)[:, None, :], (cells, 8, LANES)
                )
                return carry
            lax.fori_loop(0, 27, widen, 0)
        local_gram(s)
        if s >= 1:
            gram_over_gx(s - 1)
        if s >= 2:
            factor_block(s - 2)
        wait_halo(s)
        build_shifted(s)
        apply_operator(s)

    last = BLOCKS - 1
    local_gram(last)
    gram_over_gx(last - 1)
    factor_block(last - 2)
    apply_block(0)
    gram_over_gx(last)
    apply_block(1)
    apply_block(2)
    factor_block(last - 1)
    apply_block(last - 1)
    factor_block(last)
    apply_block(last)

    for s in range(STEPS):
        finish_halo(s)
    for j in range(BLOCKS):
        finish_gram(j)
        store(j).wait()


def local(nx, ny, right_sides, coefficients):
    rhs, nz, rows, columns = right_sides.shape
    cells = nz * rows
    total = BLOCKS * rhs
    f32 = jnp.float32
    solved, lower = pl.pallas_call(
        functools.partial(kernel, nx, ny, rhs, nz, rows, nx * ny * cells * columns),
        out_shape=(
            jax.ShapeDtypeStruct((total * cells, columns), f32),
            jax.ShapeDtypeStruct((total, LANES), f32),
        ),
        in_specs=[pl.BlockSpec(memory_space=pl.ANY)] * 2,
        out_specs=(pl.BlockSpec(memory_space=pl.ANY), pl.BlockSpec(memory_space=pltpu.VMEM)),
        scratch_shapes=[
            pltpu.VMEM((rhs * cells, columns), f32),
            pltpu.VMEM((27 * cells, columns), f32),
            pltpu.VMEM((27, cells, 8, LANES), f32),
            pltpu.VMEM((total, cells * LANES), f32),
            pltpu.VMEM((STEPS, nz, rows, rhs, LANES), f32),
            pltpu.VMEM((STEPS, 2, nz, rhs, LANES), f32),
            pltpu.VMEM((STEPS, 2, rhs, LANES), f32),
            pltpu.VMEM((STEPS, 2, 3, rhs, LANES), f32),
            pltpu.VMEM((3, nz, rows + 2, rhs, LANES), f32),
            pltpu.VMEM((BLOCKS, nx, rhs, LANES), f32),
            pltpu.VMEM((BLOCKS, ny, rhs, LANES), f32),
            pltpu.VMEM((LANES, LANES), f32),
            pltpu.VMEM((BLOCKS, rhs * cells, LANES), f32),
            pltpu.SemaphoreType.DMA((2,)),
            pltpu.SemaphoreType.DMA((BLOCKS,)),
            pltpu.SemaphoreType.DMA((STEPS, 8)),
            pltpu.SemaphoreType.DMA((STEPS, 8)),
            pltpu.SemaphoreType.DMA((BLOCKS, nx)),
            pltpu.SemaphoreType.DMA((BLOCKS, nx)),
            pltpu.SemaphoreType.DMA((BLOCKS, ny)),
            pltpu.SemaphoreType.DMA((BLOCKS, ny)),
        ],
        compiler_params=pltpu.CompilerParams(
            collective_id=0, has_side_effects=True, vmem_limit_bytes=40 * 1024 * 1024
        ),
    )(right_sides.reshape(rhs * cells, columns), coefficients.reshape(27 * cells, columns))
    return solved.reshape(total, nz, rows, columns), lower[:, :total].T


def solution(mesh):
    placed = (P(None, None, "gx", "gy"), P(None, None, "gx", "gy"))
    return jax.shard_map(
        functools.partial(local, mesh.shape["gx"], mesh.shape["gy"]),
        mesh=mesh,
        in_specs=placed,
        out_specs=(P(None, None, "gx", "gy"), P()),
        check_vma=False,
    )
```

```python
import functools

import jax
import jax.numpy as jnp
from jax import lax
from jax.experimental import pallas as pl
from jax.experimental.pallas import tpu as pltpu
from jax.sharding import PartitionSpec as P

MESH = pl.DeviceIdType.MESH
STEPS = 4
BLOCKS = STEPS + 1
LANES = 128
SIDES = (0, 1)
NT = (((1,), (1,)), ((), ()))
NN = (((1,), (0,)), ((), ()))


def split(value):
    high = value.astype(jnp.bfloat16)
    return high, (value - high.astype(jnp.float32)).astype(jnp.bfloat16)


def product(a, b, dims):
    rows = a[0].shape[0]
    both = lax.dot_general(
        jnp.concatenate(a, axis=0), b[0], dims, preferred_element_type=jnp.float32
    )
    cross = lax.dot_general(a[0], b[1], dims, preferred_element_type=jnp.float32)
    return both[:rows] + (both[rows:] + cross)


def each(start, stop, body):
    if stop - start <= 8:
        for i in range(start, stop):
            body(i)
    else:
        lax.fori_loop(start, stop, lambda i, c: (body(i), c)[1], 0)


def reciprocal(value):
    guess = pl.reciprocal(value, approx=True)
    guess = guess * (2.0 - value * guess)
    return guess * (2.0 - value * guess)


def inverse_root(value):
    guess = lax.rsqrt(value)
    return guess * (1.5 - 0.5 * value * guess * guess)


def eliminate(work, at, rhs):
    shape = work.shape
    row = lax.broadcasted_iota(jnp.int32, shape, 0)
    scale = jnp.zeros(shape, jnp.float32)
    ratio = jnp.zeros(shape, jnp.float32)
    for k in range(0, rhs, 2):
        col0 = jnp.broadcast_to(work[:, at + k : at + k + 1], shape)
        col1 = jnp.broadcast_to(work[:, at + k + 1 : at + k + 2], shape)
        row0 = jnp.broadcast_to(work[k : k + 1, :], shape)
        row1 = jnp.broadcast_to(work[k + 1 : k + 2, :], shape)
        a = jnp.broadcast_to(col0[k : k + 1, :], shape)
        b = jnp.broadcast_to(col1[k : k + 1, :], shape)
        c = jnp.broadcast_to(col1[k + 1 : k + 2, :], shape)
        over = jnp.where(row > k + 1, reciprocal(a * c - b * b), 0.0)
        slope = b * reciprocal(a)
        ratio = jnp.where(row == k + 1, slope, ratio)
        scale = jnp.where(row == k, inverse_root(a), scale)
        scale = jnp.where(row == k + 1, inverse_root(c - b * slope), scale)
        work = work - ((c * col0 - b * col1) * row0 + (a * col1 - b * col0) * row1) * over
    return (work - ratio * pltpu.roll(work, 1, 0)) * scale


def factor_rows(gram, known, at, rhs, total):
    row = lax.broadcasted_iota(jnp.int32, (rhs, LANES), 0)
    lane = lax.broadcasted_iota(jnp.int32, (rhs, LANES), 1)
    square = pltpu.roll(gram, total - at, 1) if total > at else gram
    unit = jnp.where(lane == at + row, 1.0, 0.0)
    if at:
        known = split(known)
        panel = product(split(gram), known, NT)
        halves = split(panel)
        done = product(halves, halves, NT)
        done = jnp.concatenate([done, jnp.zeros((rhs, LANES - rhs), jnp.float32)], axis=1)
        square = square - pltpu.roll(done, total, 1)
        unit = unit - product(halves, known, NN)
    else:
        panel = jnp.zeros((rhs, LANES), jnp.float32)
    work = eliminate(jnp.where(lane < total, unit, square), total, rhs)
    inverse = jnp.where(lane < total, work, 0.0)
    upper = jnp.where((lane >= total + row) & (lane < total + rhs), work, 0.0)
    return panel, inverse, pltpu.roll(upper, LANES - total + at, 1)


def put_rows(inverse_rows, high, low, out, cells):
    rhs = inverse_rows.shape[0]
    solved = product(split(inverse_rows), (high, low), NN)
    for number in range(cells):
        out[pl.ds(number, rhs, stride=cells), :] = solved[:, number * LANES : (number + 1) * LANES]


def kernel(
    nx, ny, rhs, nz, rows, total_cells,
    v_hbm, c_hbm, high, low, out, last_gram, lower_inv, panels, upper,
    v_in, c_in, wide, tile, ghost, packed, landed, shifted, gram_x, gram_y,
    load_sem, halo_send, halo_recv, gx_send, gx_recv, gy_send, gy_recv,
):
    gx, gy = lax.axis_index("gx"), lax.axis_index("gy")
    cells = nz * rows
    up, down = lax.rem(gx + 1, nx), lax.rem(gx + nx - 1, nx)
    has_left, has_right = gy > 0, gy < ny - 1
    around = (down, gx, up)
    there = (gy - 1, gy + 1)
    present = (has_left, has_right)

    load_v = pltpu.make_async_copy(v_hbm, v_in, load_sem.at[0])
    load_c = pltpu.make_async_copy(c_hbm, c_in, load_sem.at[1])
    load_v.start()
    load_c.start()

    barrier = pltpu.get_barrier_semaphore()

    def greet(x, y):
        pl.semaphore_signal(barrier, inc=1, device_id={"gx": x, "gy": y}, device_id_type=MESH)

    each(1, nx, lambda i: greet(lax.rem(gx + i, nx), gy))
    each(1, ny, lambda i: greet(gx, lax.rem(gy + i, ny)))
    for side in SIDES:
        @pl.when(present[side])
        def _():
            greet(down, there[side])
            greet(up, there[side])
    corners = 2 * has_left.astype(jnp.int32) + 2 * has_right.astype(jnp.int32)
    pl.semaphore_wait(barrier, (nx - 1) + (ny - 1) + corners)

    lane = lax.broadcasted_iota(jnp.int32, (rhs, LANES), 1)

    for side in SIDES:
        @pl.when(jnp.logical_not(present[side]))
        def _():
            for s in range(STEPS):
                landed[s, side] = jnp.zeros((3, rhs, LANES), jnp.float32)

    lower_inv[...] = jnp.zeros_like(lower_inv)
    panels[...] = jnp.zeros_like(panels)
    upper[...] = jnp.zeros_like(upper)

    def keep(j, number, value):
        at = pl.ds(number * LANES, LANES)
        high[pl.ds(j * rhs, rhs), at], low[pl.ds(j * rhs, rhs), at] = split(value)

    def row_copy(s, side):
        return pltpu.make_async_remote_copy(
            src_ref=tile.at[s, :, rows - 1 if side == 0 else 0],
            dst_ref=ghost.at[s, side],
            send_sem=halo_send.at[s, side],
            recv_sem=halo_recv.at[s, side],
            device_id={"gx": up if side == 0 else down, "gy": gy},
            device_id_type=MESH,
        )

    def column_copy(s, side, slot):
        return pltpu.make_async_remote_copy(
            src_ref=packed.at[s, side],
            dst_ref=landed.at[s, side, slot],
            send_sem=halo_send.at[s, 2 + 3 * side + slot],
            recv_sem=halo_recv.at[s, 2 + 3 * side + slot],
            device_id={"gx": around[2 - slot], "gy": there[1 - side]},
            device_id_type=MESH,
        )

    def send_halo(s):
        for side in SIDES:
            row_copy(s, side).start()
        right = jnp.zeros((rhs, LANES), jnp.float32)
        left = jnp.zeros((rhs, LANES), jnp.float32)
        for number in range(cells):
            value = tile[s, number // rows, number % rows]
            right = jnp.where(lane == number, pltpu.roll(value, number + 1, 1), right)
            moved = pltpu.roll(value, number, 1) if number else value
            left = jnp.where(lane == number, moved, left)
        packed[s, 0] = right
        packed[s, 1] = left
        for side in SIDES:
            @pl.when(present[1 - side])
            def _():
                for slot in range(3):
                    column_copy(s, side, slot).start()

    def wait_halo(s):
        for side in SIDES:
            row_copy(s, side).wait_recv()
        for side in SIDES:
            @pl.when(present[side])
            def _():
                for slot in range(3):
                    column_copy(s, side, slot).wait_recv()

    def finish_halo(s):
        for side in SIDES:
            row_copy(s, side).wait_send()
            @pl.when(present[1 - side])
            def _():
                for slot in range(3):
                    column_copy(s, side, slot).wait_send()

    def build_shifted(s):
        for padded in range(rows + 2):
            slot = 0 if padded == 0 else 2 if padded == rows + 1 else 1
            before, after = landed[s, 0, slot], landed[s, 1, slot]
            x = (padded - 1) % rows
            for z in range(nz):
                if slot == 1:
                    value = tile[s, z, x]
                else:
                    value = ghost[s, slot // 2, z]
                number = z * rows + x
                edge = pltpu.roll(before, LANES - 1 - number, 1)
                shifted[0, z, padded] = pltpu.roll(jnp.where(lane == LANES - 1, edge, value), 1, 1)
                shifted[1, z, padded] = value
                edge = pltpu.roll(after, LANES - number, 1) if number else after
                shifted[2, z, padded] = pltpu.roll(jnp.where(lane == 0, edge, value), LANES - 1, 1)

    def apply_operator(s):
        for z in range(nz):
            total = jnp.zeros((rows, rhs // 8, 8, LANES), jnp.float32)
            for dz in (-1, 0, 1):
                if not 0 <= z + dz < nz:
                    continue
                for dx in (-1, 0, 1):
                    for dy in (-1, 0, 1):
                        number = 9 * (dz + 1) + 3 * (dx + 1) + (dy + 1)
                        weight = wide[number, z * rows : (z + 1) * rows]
                        window = shifted[dy + 1, z + dz, 1 + dx : 1 + dx + rows]
                        total = total + weight[:, None] * window.reshape(total.shape)
            total = total.reshape(rows, rhs, LANES)
            for x in range(rows):
                value = total[x]
                if s > 0:
                    value = 2.0 * value - tile[s - 1, z, x]
                keep(s + 1, z * rows + x, value)
                if s + 1 < STEPS:
                    tile[s + 1, z, x] = value

    def gx_copy(j, slot, x):
        return pltpu.make_async_remote_copy(
            src_ref=gram_x.at[j, slot], dst_ref=gram_x.at[j, slot],
            send_sem=gx_send.at[j, x], recv_sem=gx_recv.at[j, slot],
            device_id={"gx": x, "gy": gy}, device_id_type=MESH,
        )

    def gy_copy(j, slot, y):
        return pltpu.make_async_remote_copy(
            src_ref=gram_y.at[j, slot], dst_ref=gram_y.at[j, slot],
            send_sem=gy_send.at[j, y], recv_sem=gy_recv.at[j, slot],
            device_id={"gx": gx, "gy": y}, device_id_type=MESH,
        )

    def local_gram(j):
        upto = (j + 1) * rhs
        here = slice(j * rhs, upto)
        part = product((high[here, :], low[here, :]), (high[0:upto, :], low[0:upto, :]), NT)
        gram_x[j, gx] = jnp.concatenate(
            [part, jnp.zeros((rhs, LANES - upto), jnp.float32)], axis=1
        )
        def go(i):
            gx_copy(j, gx, lax.rem(gx + i, nx)).start()
        each(1, nx, go)

    def gram_over_gx(j):
        def wait(i):
            other = lax.rem(gx + i, nx)
            gx_copy(j, other, other).wait_recv()
        each(1, nx, wait)
        gram_y[j, gy] = jnp.sum(gram_x[j], axis=0)
        def go(i):
            gy_copy(j, gy, lax.rem(gy + i, ny)).start()
        each(1, ny, go)

    def gram_over_gy(j):
        def wait(i):
            other = lax.rem(gy + i, ny)
            gy_copy(j, other, other).wait_recv()
        each(1, ny, wait)
        return jnp.sum(gram_y[j], axis=0) / jnp.float32(total_cells)

    def finish_gram(j):
        def done_x(i):
            gx_copy(j, gx, lax.rem(gx + i, nx)).wait_send()
        each(1, nx, done_x)
        def done_y(i):
            gy_copy(j, gy, lax.rem(gy + i, ny)).wait_send()
        each(1, ny, done_y)

    def factor_block(j):
        at = j * rhs
        here = slice(at, at + rhs)
        panel, inverse, diagonal = factor_rows(
            gram_over_gy(j), lower_inv[...], at, rhs, BLOCKS * rhs
        )
        panels[here, :] = panel
        lower_inv[here, :] = inverse
        upper[here, :] = diagonal

    def apply_block(j):
        at, upto = j * rhs, (j + 1) * rhs
        put_rows(lower_inv[at:upto, 0:upto], high[0:upto, :], low[0:upto, :], out.at[j], cells)

    load_v.wait()
    for number in range(cells):
        value = v_in[pl.ds(number, rhs, stride=cells), :]
        tile[0, number // rows, number % rows] = value
        keep(0, number, value)

    for s in range(STEPS):
        send_halo(s)
        if s == 0:
            load_c.wait()
            def widen(number, carry):
                values = c_in[pl.ds(number * cells, cells), :]
                center = jnp.where(number == 13, 3.0, 0.0)
                wide[number] = jnp.broadcast_to(
                    (2.0 * values - center)[:, None, :], (cells, 8, LANES)
                )
                return carry
            lax.fori_loop(0, 27, widen, 0)
        local_gram(s)
        if s >= 1:
            gram_over_gx(s - 1)
        if s >= 2:
            factor_block(s - 2)
        wait_halo(s)
        build_shifted(s)
        apply_operator(s)

    last = BLOCKS - 1
    local_gram(last)
    gram_over_gx(last - 1)
    factor_block(last - 2)
    apply_block(0)
    gram_over_gx(last)
    apply_block(1)
    apply_block(2)
    factor_block(last - 1)
    apply_block(last - 1)
    last_gram[...] = gram_over_gy(last)

    for s in range(STEPS):
        finish_halo(s)
    for j in range(BLOCKS):
        finish_gram(j)


def finish_kernel(
    rhs, cells, high, low, first, last_gram, lower_inv, panels, upper, q_hbm, r_hbm,
    out, square, sem,
):
    total, last = BLOCKS * rhs, BLOCKS - 1
    store_first = pltpu.make_async_copy(first, q_hbm.at[pl.ds(0, last), :, :], sem.at[0])
    store_last = pltpu.make_async_copy(out, q_hbm.at[last], sem.at[1])
    store_square = pltpu.make_async_copy(square, r_hbm, sem.at[2])
    store_first.start()
    at = last * rhs
    panel, inverse, diagonal = factor_rows(last_gram[...], lower_inv[...], at, rhs, total)
    put_rows(inverse[:, 0:total], high[...], low[...], out, cells)
    store_last.start()
    pad = jnp.zeros((LANES - total, LANES), jnp.float32)
    lower = jnp.concatenate([panels[0:at, :], panel, pad], axis=0)
    diagonals = jnp.concatenate([upper[0:at, :], diagonal, pad], axis=0)
    square[...] = (jnp.transpose(lower) + diagonals)[0:total, 0:total]
    store_square.start()
    store_first.wait()
    store_last.wait()
    store_square.wait()


def local(nx, ny, right_sides, coefficients):
    rhs, nz, rows, columns = right_sides.shape
    cells = nz * rows
    total = BLOCKS * rhs
    size = rhs * cells
    f32, b16 = jnp.float32, jnp.bfloat16
    vmem = pl.BlockSpec(memory_space=pltpu.VMEM)
    hbm = pl.BlockSpec(memory_space=pltpu.HBM)
    shape = jax.ShapeDtypeStruct
    parts = pl.pallas_call(
        functools.partial(kernel, nx, ny, rhs, nz, rows, nx * ny * cells * columns),
        out_shape=(
            shape((total, cells * LANES), b16),
            shape((total, cells * LANES), b16),
            shape((BLOCKS - 1, size, columns), f32),
            shape((rhs, LANES), f32),
            shape((LANES, LANES), f32),
            shape((total, LANES), f32),
            shape((total, LANES), f32),
        ),
        in_specs=[hbm] * 2,
        out_specs=(vmem,) * 7,
        scratch_shapes=[
            pltpu.VMEM((size, columns), f32),
            pltpu.VMEM((27 * cells, columns), f32),
            pltpu.VMEM((27, cells, 8, LANES), f32),
            pltpu.VMEM((STEPS, nz, rows, rhs, LANES), f32),
            pltpu.VMEM((STEPS, 2, nz, rhs, LANES), f32),
            pltpu.VMEM((STEPS, 2, rhs, LANES), f32),
            pltpu.VMEM((STEPS, 2, 3, rhs, LANES), f32),
            pltpu.VMEM((3, nz, rows + 2, rhs, LANES), f32),
            pltpu.VMEM((BLOCKS, nx, rhs, LANES), f32),
            pltpu.VMEM((BLOCKS, ny, rhs, LANES), f32),
            pltpu.SemaphoreType.DMA((2,)),
            pltpu.SemaphoreType.DMA((STEPS, 8)),
            pltpu.SemaphoreType.DMA((STEPS, 8)),
            pltpu.SemaphoreType.DMA((BLOCKS, nx)),
            pltpu.SemaphoreType.DMA((BLOCKS, nx)),
            pltpu.SemaphoreType.DMA((BLOCKS, ny)),
            pltpu.SemaphoreType.DMA((BLOCKS, ny)),
        ],
        compiler_params=pltpu.CompilerParams(
            collective_id=0, has_side_effects=True, vmem_limit_bytes=32 * 1024 * 1024
        ),
    )(
        pltpu.with_memory_space_constraint(right_sides.reshape(size, columns), pltpu.HBM),
        pltpu.with_memory_space_constraint(coefficients.reshape(27 * cells, columns), pltpu.HBM),
    )
    solved, square = pl.pallas_call(
        functools.partial(finish_kernel, rhs, cells),
        out_shape=(shape((BLOCKS, size, columns), f32), shape((total, total), f32)),
        in_specs=[vmem] * 7,
        out_specs=(hbm, hbm),
        scratch_shapes=[
            pltpu.VMEM((size, columns), f32),
            pltpu.VMEM((total, total), f32),
            pltpu.SemaphoreType.DMA((3,)),
        ],
        compiler_params=pltpu.CompilerParams(vmem_limit_bytes=16 * 1024 * 1024),
    )(*parts)
    return solved.reshape(total, nz, rows, columns), square


def solution(mesh):
    placed = (P(None, None, "gx", "gy"), P(None, None, "gx", "gy"))
    return jax.shard_map(
        functools.partial(local, mesh.shape["gx"], mesh.shape["gy"]),
        mesh=mesh,
        in_specs=placed,
        out_specs=(P(None, None, "gx", "gy"), P()),
        check_vma=False,
    )
```

```python
import functools

import jax
import jax.numpy as jnp
from jax import lax
from jax.experimental import pallas as pl
from jax.experimental.pallas import tpu as pltpu
from jax.sharding import PartitionSpec as P

MESH = pl.DeviceIdType.MESH
STEPS = 4
BLOCKS = STEPS + 1
LANES = 128
SIDES = (0, 1)
NT = (((1,), (1,)), ((), ()))
NN = (((1,), (0,)), ((), ()))


def split(value):
    high = value.astype(jnp.bfloat16)
    return high, (value - high.astype(jnp.float32)).astype(jnp.bfloat16)


def product(a, b, dims):
    rows = a[0].shape[0]
    both = lax.dot_general(
        jnp.concatenate(a, axis=0), b[0], dims, preferred_element_type=jnp.float32
    )
    cross = lax.dot_general(a[0], b[1], dims, preferred_element_type=jnp.float32)
    return both[:rows] + (both[rows:] + cross)


def each(start, stop, body):
    if stop - start <= 8:
        for i in range(start, stop):
            body(i)
    else:
        lax.fori_loop(start, stop, lambda i, c: (body(i), c)[1], 0)


def reciprocal(value):
    guess = pl.reciprocal(value, approx=True)
    guess = guess * (2.0 - value * guess)
    return guess * (2.0 - value * guess)


def inverse_root(value):
    guess = lax.rsqrt(value)
    return guess * (1.5 - 0.5 * value * guess * guess)


def eliminate(work, at, rhs):
    shape = work.shape
    row = lax.broadcasted_iota(jnp.int32, shape, 0)
    scale = jnp.zeros(shape, jnp.float32)
    ratio = jnp.zeros(shape, jnp.float32)
    for k in range(0, rhs, 2):
        col0 = jnp.broadcast_to(work[:, at + k : at + k + 1], shape)
        col1 = jnp.broadcast_to(work[:, at + k + 1 : at + k + 2], shape)
        row0 = jnp.broadcast_to(work[k : k + 1, :], shape)
        row1 = jnp.broadcast_to(work[k + 1 : k + 2, :], shape)
        a = jnp.broadcast_to(col0[k : k + 1, :], shape)
        b = jnp.broadcast_to(col1[k : k + 1, :], shape)
        c = jnp.broadcast_to(col1[k + 1 : k + 2, :], shape)
        over = jnp.where(row > k + 1, reciprocal(a * c - b * b), 0.0)
        slope = b * reciprocal(a)
        ratio = jnp.where(row == k + 1, slope, ratio)
        scale = jnp.where(row == k, inverse_root(a), scale)
        scale = jnp.where(row == k + 1, inverse_root(c - b * slope), scale)
        work = work - ((c * col0 - b * col1) * row0 + (a * col1 - b * col0) * row1) * over
    return (work - ratio * pltpu.roll(work, 1, 0)) * scale


def factor_rows(gram, known, at, rhs, total):
    row = lax.broadcasted_iota(jnp.int32, (rhs, LANES), 0)
    lane = lax.broadcasted_iota(jnp.int32, (rhs, LANES), 1)
    square = pltpu.roll(gram, total - at, 1) if total > at else gram
    unit = jnp.where(lane == at + row, 1.0, 0.0)
    if at:
        known = split(known)
        panel = product(split(gram), known, NT)
        halves = split(panel)
        done = product(halves, halves, NT)
        done = jnp.concatenate([done, jnp.zeros((rhs, LANES - rhs), jnp.float32)], axis=1)
        square = square - pltpu.roll(done, total, 1)
        unit = unit - product(halves, known, NN)
    else:
        panel = jnp.zeros((rhs, LANES), jnp.float32)
    work = eliminate(jnp.where(lane < total, unit, square), total, rhs)
    inverse = jnp.where(lane < total, work, 0.0)
    upper = jnp.where((lane >= total + row) & (lane < total + rhs), work, 0.0)
    return panel, inverse, pltpu.roll(upper, LANES - total + at, 1)


def put_rows(inverse_rows, high, low, out, cells):
    rhs = inverse_rows.shape[0]
    solved = product(split(inverse_rows), (high, low), NN)
    for number in range(cells):
        out[pl.ds(number, rhs, stride=cells), :] = solved[:, number * LANES : (number + 1) * LANES]


def turn(value, shift):
    shift %= LANES
    return pltpu.roll(value, shift, 1) if shift else value


def lanes_of(value):
    return lax.broadcasted_iota(jnp.int32, value.shape, 1)


def edge_windows(value, left, right, number):
    lane = lanes_of(value)
    result = jnp.where(lane < 16, turn(right, 12 - 4 * number), 0.0)
    result = jnp.where(lane < 12, turn(value, 12), result)
    result = jnp.where(lane < 8, turn(value, 4), result)
    return jnp.where(lane < 4, turn(left, -4 * number), result)


def pack_edges(values):
    lane = lanes_of(values[0])
    last = first = jnp.zeros(values[0].shape, jnp.float32)
    for number, value in enumerate(values):
        mine = (lane >= 4 * number) & (lane < 4 * number + 4)
        last = jnp.where(mine, turn(value, 4 * number + 4), last)
        first = jnp.where(mine, turn(value, 4 * number), first)
    return last, first


def kernel(
    nx, ny, rhs, nz, rows, total_cells,
    v_hbm, c_hbm, high, low, out, last_gram, lower_inv, panels, upper,
    v_in, c_in, wide, wide_edge, tile, edge, ghost, packed, landed, packed_c, landed_c,
    packed_edge, ghost_edge, shifted, shifted_edge, gram_x, gram_y,
    load_sem, halo_send, halo_recv, coef_send, coef_recv, gx_send, gx_recv, gy_send, gy_recv,
):
    gx, gy = lax.axis_index("gx"), lax.axis_index("gy")
    cells = nz * rows
    up, down = lax.rem(gx + 1, nx), lax.rem(gx + nx - 1, nx)
    has_left, has_right = gy > 0, gy < ny - 1
    around = (down, gx, up)
    there = (gy - 1, gy + 1)
    present = (has_left, has_right)

    load_v = pltpu.make_async_copy(v_hbm, v_in, load_sem.at[0])
    load_c = pltpu.make_async_copy(c_hbm, c_in, load_sem.at[1])
    load_v.start()
    load_c.start()

    pair, place = gy // 2, gy % 2
    plane, planes = 2 * gx + place, 2 * nx
    pairs = ny // 2

    def in_plane(i):
        other = lax.rem(plane + i, planes)
        return other, {"gx": other // 2, "gy": 2 * pair + other % 2}

    def in_line(i):
        other = lax.rem(pair + i, pairs)
        return other, {"gx": gx, "gy": 2 * other + place}

    barrier = pltpu.get_barrier_semaphore()

    def greet(device):
        pl.semaphore_signal(barrier, inc=1, device_id=device, device_id_type=MESH)

    across = gy + 2 * place - 1
    has_across = (across >= 0) & (across < ny)

    @pl.when(has_across)
    def _():
        for x in around:
            greet({"gx": x, "gy": across})
    each(1, pairs, lambda i: greet(in_line(i)[1]))
    each(1, planes, lambda i: greet(in_plane(i)[1]))

    lane = lax.broadcasted_iota(jnp.int32, (rhs, LANES), 1)

    for side in SIDES:
        @pl.when(jnp.logical_not(present[side]))
        def _():
            landed[side] = jnp.zeros((3, rhs, LANES), jnp.float32)
            landed_c[side] = jnp.zeros((cells, LANES), jnp.float32)

    lower_inv[...] = jnp.zeros_like(lower_inv)
    panels[...] = jnp.zeros_like(panels)
    upper[...] = jnp.zeros_like(upper)

    def keep(j, number, value):
        at = pl.ds(number * LANES, LANES)
        high[pl.ds(j * rhs, rhs), at], low[pl.ds(j * rhs, rhs), at] = split(value)

    def row_copy(s, side):
        return pltpu.make_async_remote_copy(
            src_ref=tile.at[s, :, rows - 1 if side == 0 else 0],
            dst_ref=ghost.at[s, side],
            send_sem=halo_send.at[s, side],
            recv_sem=halo_recv.at[s, side],
            device_id={"gx": up if side == 0 else down, "gy": gy},
            device_id_type=MESH,
        )

    def column_copy(side, slot):
        return pltpu.make_async_remote_copy(
            src_ref=packed.at[side],
            dst_ref=landed.at[side, slot],
            send_sem=halo_send.at[0, 2 + 3 * side + slot],
            recv_sem=halo_recv.at[0, 2 + 3 * side + slot],
            device_id={"gx": around[2 - slot], "gy": there[1 - side]},
            device_id_type=MESH,
        )

    def coefficient_copy(side):
        return pltpu.make_async_remote_copy(
            src_ref=packed_c.at[side],
            dst_ref=landed_c.at[side],
            send_sem=coef_send.at[side],
            recv_sem=coef_recv.at[side],
            device_id={"gx": gx, "gy": there[1 - side]},
            device_id_type=MESH,
        )

    def edge_copy(s, side):
        return pltpu.make_async_remote_copy(
            src_ref=packed_edge.at[s, side],
            dst_ref=ghost_edge.at[s, side],
            send_sem=halo_send.at[s, 2 + side],
            recv_sem=halo_recv.at[s, 2 + side],
            device_id={"gx": up if side == 0 else down, "gy": gy},
            device_id_type=MESH,
        )

    def send_rows(s):
        for side in SIDES:
            row_copy(s, side).start()

    def send_edges(s):
        lane8 = lax.broadcasted_iota(jnp.int32, (8, LANES), 1)
        for side in SIDES:
            x = rows - 1 if side == 0 else 0
            held = jnp.zeros((8, LANES), jnp.float32)
            for z in range(nz):
                for half in range(rhs // 8):
                    at = 16 * (z * (rhs // 8) + half)
                    value = edge[s, z, x, 8 * half : 8 * half + 8, :]
                    held = jnp.where((lane8 >= at) & (lane8 < at + 16), turn(value, at), held)
            packed_edge[s, side] = held
            edge_copy(s, side).start()

    def ghost_edge_tile(s, side, z):
        if s == 0:
            slot = 2 * side
            number = z * rows + (rows - 1 if side == 0 else 0)
            return edge_windows(ghost[0, side, z], landed[0, slot], landed[1, slot], number)
        held = ghost_edge[s, side]
        per = rhs // 8
        parts = [turn(held, -16 * (z * per + half)) for half in range(per)]
        return jnp.concatenate(parts, axis=0)

    def build_shifted(s):
        for padded in range(rows + 2):
            x = padded - 1
            for z in range(nz):
                if 0 <= x < rows:
                    value, window = tile[s, z, x], edge[s, z, x]
                else:
                    side = 0 if x < 0 else 1
                    value, window = ghost[s, side, z], ghost_edge_tile(s, side, z)
                shifted[0, z, padded] = jnp.where(lane == 0, turn(window, -3), turn(value, 1))
                shifted[1, z, padded] = value
                shifted[2, z, padded] = jnp.where(
                    lane == LANES - 1, turn(window, LANES - 13), turn(value, -1)
                )
                if s + 1 < STEPS:
                    shifted_edge[0, z, padded] = turn(window, 1)
                    shifted_edge[1, z, padded] = window
                    shifted_edge[2, z, padded] = turn(window, -1)

    def apply_operator(s, weights, moved, held, main):
        for z in range(nz):
            total = jnp.zeros((rows, rhs // 8, 8, LANES), jnp.float32)
            for dz in (-1, 0, 1):
                if not 0 <= z + dz < nz:
                    continue
                for dx in (-1, 0, 1):
                    for dy in (-1, 0, 1):
                        number = 9 * (dz + 1) + 3 * (dx + 1) + (dy + 1)
                        weight = weights[number, z * rows : (z + 1) * rows]
                        window = moved[dy + 1, z + dz, 1 + dx : 1 + dx + rows]
                        total = total + weight[:, None] * window.reshape(total.shape)
            total = total.reshape(rows, rhs, LANES)
            for x in range(rows):
                value = total[x]
                if s > 0:
                    value = 2.0 * value - held[s - 1, z, x]
                if main:
                    keep(s + 1, z * rows + x, value)
                if s + 1 < STEPS:
                    held[s + 1, z, x] = value

    def gx_copy(j, slot, other, device):
        return pltpu.make_async_remote_copy(
            src_ref=gram_x.at[j, slot], dst_ref=gram_x.at[j, slot],
            send_sem=gx_send.at[j, other], recv_sem=gx_recv.at[j, slot],
            device_id=device, device_id_type=MESH,
        )

    def gy_copy(j, slot, other, device):
        return pltpu.make_async_remote_copy(
            src_ref=gram_y.at[j, slot], dst_ref=gram_y.at[j, slot],
            send_sem=gy_send.at[j, other], recv_sem=gy_recv.at[j, slot],
            device_id=device, device_id_type=MESH,
        )

    def local_gram(j):
        upto = (j + 1) * rhs
        here = slice(j * rhs, upto)
        part = product((high[here, :], low[here, :]), (high[0:upto, :], low[0:upto, :]), NT)
        gram_x[j, plane] = jnp.concatenate(
            [part, jnp.zeros((rhs, LANES - upto), jnp.float32)], axis=1
        )
        def go(i):
            gx_copy(j, plane, *in_plane(i)).start()
        each(1, planes, go)

    def gram_over_gx(j):
        def wait(i):
            other, device = in_plane(i)
            gx_copy(j, other, other, device).wait_recv()
        each(1, planes, wait)
        gram_y[j, pair] = jnp.sum(gram_x[j], axis=0)
        def go(i):
            gy_copy(j, pair, *in_line(i)).start()
        each(1, pairs, go)

    def gram_over_gy(j):
        def wait(i):
            other, device = in_line(i)
            gy_copy(j, other, other, device).wait_recv()
        each(1, pairs, wait)
        return jnp.sum(gram_y[j], axis=0) / jnp.float32(total_cells)

    def finish_gram(j):
        def done_x(i):
            gx_copy(j, plane, *in_plane(i)).wait_send()
        each(1, planes, done_x)
        def done_y(i):
            gy_copy(j, pair, *in_line(i)).wait_send()
        each(1, pairs, done_y)

    def factor_block(j):
        at = j * rhs
        here = slice(at, at + rhs)
        panel, inverse, diagonal = factor_rows(
            gram_over_gy(j), lower_inv[...], at, rhs, BLOCKS * rhs
        )
        panels[here, :] = panel
        lower_inv[here, :] = inverse
        upper[here, :] = diagonal

    def apply_block(j):
        at, upto = j * rhs, (j + 1) * rhs
        put_rows(lower_inv[at:upto, 0:upto], high[0:upto, :], low[0:upto, :], out.at[j], cells)

    load_v.wait()
    values = []
    for number in range(cells):
        value = v_in[pl.ds(number, rhs, stride=cells), :]
        tile[0, number // rows, number % rows] = value
        keep(0, number, value)
        values.append(value)
    packed[0], packed[1] = pack_edges(values)

    def weights_of(number):
        return 2.0 * c_in[number * cells : (number + 1) * cells, :] - (3.0 if number == 13 else 0.0)

    load_c.wait()
    packed_c[0], packed_c[1] = pack_edges([weights_of(number) for number in range(27)])
    pl.semaphore_wait(
        barrier, (planes - 1) + (pairs - 1) + 3 * has_across.astype(jnp.int32)
    )
    send_rows(0)
    for side in SIDES:
        @pl.when(present[1 - side])
        def _():
            for slot in range(3):
                column_copy(side, slot).start()
            coefficient_copy(side).start()
    for number in range(27):
        wide[number] = jnp.broadcast_to(weights_of(number)[:, None, :], (cells, 8, LANES))

    for s in range(STEPS):
        local_gram(s)
        if s >= 1:
            gram_over_gx(s - 1)
        if s >= 2:
            factor_block(s - 2)
        for side in SIDES:
            row_copy(s, side).wait_recv()
            if s > 0:
                edge_copy(s, side).wait_recv()
        if s == 0:
            for side in SIDES:
                @pl.when(present[side])
                def _():
                    for slot in range(3):
                        column_copy(side, slot).wait_recv()
            for number in range(cells):
                z, x = number // rows, number % rows
                edge[0, z, x] = edge_windows(tile[0, z, x], landed[0, 1], landed[1, 1], number)
        build_shifted(s)
        apply_operator(s, wide, shifted, tile, True)
        if s + 1 < STEPS:
            send_rows(s + 1)
            if s == 0:
                for side in SIDES:
                    @pl.when(present[side])
                    def _():
                        coefficient_copy(side).wait_recv()
                for number in range(27):
                    weight = edge_windows(
                        weights_of(number), landed_c[0], landed_c[1], number
                    )
                    wide_edge[number] = jnp.broadcast_to(weight[:, None, :], (cells, 8, LANES))
            apply_operator(s, wide_edge, shifted_edge, edge, False)
            send_edges(s + 1)

    last = BLOCKS - 1
    local_gram(last)
    gram_over_gx(last - 1)
    factor_block(last - 2)
    apply_block(0)
    gram_over_gx(last)
    apply_block(1)
    apply_block(2)
    factor_block(last - 1)
    apply_block(last - 1)
    last_gram[...] = gram_over_gy(last)

    for s in range(STEPS):
        for side in SIDES:
            row_copy(s, side).wait_send()
            if s > 0:
                edge_copy(s, side).wait_send()
    for side in SIDES:
        @pl.when(present[1 - side])
        def _():
            for slot in range(3):
                column_copy(side, slot).wait_send()
            coefficient_copy(side).wait_send()
    for j in range(BLOCKS):
        finish_gram(j)


def finish_kernel(
    rhs, cells, high, low, first, last_gram, lower_inv, panels, upper, q_hbm, r_hbm,
    out, square, sem,
):
    total, last = BLOCKS * rhs, BLOCKS - 1
    store_first = pltpu.make_async_copy(first, q_hbm.at[pl.ds(0, last), :, :], sem.at[0])
    store_last = pltpu.make_async_copy(out, q_hbm.at[last], sem.at[1])
    store_square = pltpu.make_async_copy(square, r_hbm, sem.at[2])
    store_first.start()
    at = last * rhs
    panel, inverse, diagonal = factor_rows(last_gram[...], lower_inv[...], at, rhs, total)
    put_rows(inverse[:, 0:total], high[...], low[...], out, cells)
    store_last.start()
    pad = jnp.zeros((LANES - total, LANES), jnp.float32)
    lower = jnp.concatenate([panels[0:at, :], panel, pad], axis=0)
    diagonals = jnp.concatenate([upper[0:at, :], diagonal, pad], axis=0)
    square[...] = (jnp.transpose(lower) + diagonals)[0:total, 0:total]
    store_square.start()
    store_first.wait()
    store_last.wait()
    store_square.wait()


def local(nx, ny, right_sides, coefficients):
    rhs, nz, rows, columns = right_sides.shape
    cells = nz * rows
    total = BLOCKS * rhs
    size = rhs * cells
    f32, b16 = jnp.float32, jnp.bfloat16
    vmem = pl.BlockSpec(memory_space=pltpu.VMEM)
    hbm = pl.BlockSpec(memory_space=pltpu.HBM)
    shape = jax.ShapeDtypeStruct
    parts = pl.pallas_call(
        functools.partial(kernel, nx, ny, rhs, nz, rows, nx * ny * cells * columns),
        out_shape=(
            shape((total, cells * LANES), b16),
            shape((total, cells * LANES), b16),
            shape((BLOCKS - 1, size, columns), f32),
            shape((rhs, LANES), f32),
            shape((LANES, LANES), f32),
            shape((total, LANES), f32),
            shape((total, LANES), f32),
        ),
        in_specs=[hbm] * 2,
        out_specs=(vmem,) * 7,
        scratch_shapes=[
            pltpu.VMEM((size, columns), f32),
            pltpu.VMEM((27 * cells, columns), f32),
            pltpu.VMEM((27, cells, 8, LANES), f32),
            pltpu.VMEM((27, cells, 8, LANES), f32),
            pltpu.VMEM((STEPS, nz, rows, rhs, LANES), f32),
            pltpu.VMEM((STEPS, nz, rows, rhs, LANES), f32),
            pltpu.VMEM((STEPS, 2, nz, rhs, LANES), f32),
            pltpu.VMEM((2, rhs, LANES), f32),
            pltpu.VMEM((2, 3, rhs, LANES), f32),
            pltpu.VMEM((2, cells, LANES), f32),
            pltpu.VMEM((2, cells, LANES), f32),
            pltpu.VMEM((STEPS, 2, 8, LANES), f32),
            pltpu.VMEM((STEPS, 2, 8, LANES), f32),
            pltpu.VMEM((3, nz, rows + 2, rhs, LANES), f32),
            pltpu.VMEM((3, nz, rows + 2, rhs, LANES), f32),
            pltpu.VMEM((BLOCKS, 2 * nx, rhs, LANES), f32),
            pltpu.VMEM((BLOCKS, ny // 2, rhs, LANES), f32),
            pltpu.SemaphoreType.DMA((2,)),
            pltpu.SemaphoreType.DMA((STEPS, 8)),
            pltpu.SemaphoreType.DMA((STEPS, 8)),
            pltpu.SemaphoreType.DMA((2,)),
            pltpu.SemaphoreType.DMA((2,)),
            pltpu.SemaphoreType.DMA((BLOCKS, 2 * nx)),
            pltpu.SemaphoreType.DMA((BLOCKS, 2 * nx)),
            pltpu.SemaphoreType.DMA((BLOCKS, ny // 2)),
            pltpu.SemaphoreType.DMA((BLOCKS, ny // 2)),
        ],
        compiler_params=pltpu.CompilerParams(
            collective_id=0, has_side_effects=True, vmem_limit_bytes=32 * 1024 * 1024
        ),
    )(
        pltpu.with_memory_space_constraint(right_sides.reshape(size, columns), pltpu.HBM),
        pltpu.with_memory_space_constraint(coefficients.reshape(27 * cells, columns), pltpu.HBM),
    )
    solved, square = pl.pallas_call(
        functools.partial(finish_kernel, rhs, cells),
        out_shape=(shape((BLOCKS, size, columns), f32), shape((total, total), f32)),
        in_specs=[vmem] * 7,
        out_specs=(hbm, hbm),
        scratch_shapes=[
            pltpu.VMEM((size, columns), f32),
            pltpu.VMEM((total, total), f32),
            pltpu.SemaphoreType.DMA((3,)),
        ],
        compiler_params=pltpu.CompilerParams(vmem_limit_bytes=16 * 1024 * 1024),
    )(*parts)
    return solved.reshape(total, nz, rows, columns), square


def solution(mesh):
    placed = (P(None, None, "gx", "gy"), P(None, None, "gx", "gy"))
    return jax.shard_map(
        functools.partial(local, mesh.shape["gx"], mesh.shape["gy"]),
        mesh=mesh,
        in_specs=placed,
        out_specs=(P(None, None, "gx", "gy"), P()),
        check_vma=False,
    )
```

```python
import functools

import jax
import jax.numpy as jnp
from jax import lax
from jax.experimental import pallas as pl
from jax.experimental.pallas import tpu as pltpu
from jax.sharding import PartitionSpec as P

MESH = pl.DeviceIdType.MESH
STEPS = 4
BLOCKS = STEPS + 1
LANES = 128
SIDES = (0, 1)
NT = (((1,), (1,)), ((), ()))
NN = (((1,), (0,)), ((), ()))
GROUPS = ((0, 2), (2, 4), (4, 5))


def split(value):
    high = value.astype(jnp.bfloat16)
    return high, (value - high.astype(jnp.float32)).astype(jnp.bfloat16)


def product(a, b, dims):
    rows = a[0].shape[0]
    both = lax.dot_general(
        jnp.concatenate(a, axis=0), b[0], dims, preferred_element_type=jnp.float32
    )
    cross = lax.dot_general(a[0], b[1], dims, preferred_element_type=jnp.float32)
    return both[:rows] + (both[rows:] + cross)


def each(start, stop, body):
    if stop - start <= 8:
        for i in range(start, stop):
            body(i)
    else:
        lax.fori_loop(start, stop, lambda i, c: (body(i), c)[1], 0)


def reciprocal(value):
    guess = pl.reciprocal(value, approx=True)
    guess = guess * (2.0 - value * guess)
    return guess * (2.0 - value * guess)


def inverse_root(value):
    guess = lax.rsqrt(value)
    return guess * (1.5 - 0.5 * value * guess * guess)


def eliminate(work, at, rhs):
    shape = work.shape
    row = lax.broadcasted_iota(jnp.int32, shape, 0)
    scale = jnp.zeros(shape, jnp.float32)
    ratio = jnp.zeros(shape, jnp.float32)
    for k in range(0, rhs, 2):
        col0 = jnp.broadcast_to(work[:, at + k : at + k + 1], shape)
        col1 = jnp.broadcast_to(work[:, at + k + 1 : at + k + 2], shape)
        row0 = jnp.broadcast_to(work[k : k + 1, :], shape)
        row1 = jnp.broadcast_to(work[k + 1 : k + 2, :], shape)
        a = jnp.broadcast_to(col0[k : k + 1, :], shape)
        b = jnp.broadcast_to(col1[k : k + 1, :], shape)
        c = jnp.broadcast_to(col1[k + 1 : k + 2, :], shape)
        over = jnp.where(row > k + 1, reciprocal(a * c - b * b), 0.0)
        slope = b * reciprocal(a)
        ratio = jnp.where(row == k + 1, slope, ratio)
        scale = jnp.where(row == k, inverse_root(a), scale)
        scale = jnp.where(row == k + 1, inverse_root(c - b * slope), scale)
        work = work - ((c * col0 - b * col1) * row0 + (a * col1 - b * col0) * row1) * over
    return (work - ratio * pltpu.roll(work, 1, 0)) * scale


def factor_rows(gram, known, at, rhs, total):
    row = lax.broadcasted_iota(jnp.int32, (rhs, LANES), 0)
    lane = lax.broadcasted_iota(jnp.int32, (rhs, LANES), 1)
    square = pltpu.roll(gram, total - at, 1) if total > at else gram
    unit = jnp.where(lane == at + row, 1.0, 0.0)
    if at:
        known = split(known)
        panel = product(split(gram), known, NT)
        halves = split(panel)
        done = product(halves, halves, NT)
        done = jnp.concatenate([done, jnp.zeros((rhs, LANES - rhs), jnp.float32)], axis=1)
        square = square - pltpu.roll(done, total, 1)
        unit = unit - product(halves, known, NN)
    else:
        panel = jnp.zeros((rhs, LANES), jnp.float32)
    work = eliminate(jnp.where(lane < total, unit, square), total, rhs)
    inverse = jnp.where(lane < total, work, 0.0)
    upper = jnp.where((lane >= total + row) & (lane < total + rhs), work, 0.0)
    return panel, inverse, pltpu.roll(upper, LANES - total + at, 1)


def put_rows(inverse_rows, high, low, out, cells):
    rhs = inverse_rows.shape[0]
    solved = product(split(inverse_rows), (high, low), NN)
    for number in range(cells):
        out[pl.ds(number, rhs, stride=cells), :] = solved[:, number * LANES : (number + 1) * LANES]


def turn(value, shift):
    shift %= LANES
    return pltpu.roll(value, shift, 1) if shift else value


def lanes_of(value):
    return lax.broadcasted_iota(jnp.int32, value.shape, 1)


def edge_own(value, shift=0):
    lane = (lanes_of(value) + (LANES - shift)) % LANES
    return jnp.where(lane < 8, turn(value, 4 + shift), turn(value, 12 + shift))


def edge_windows(own, left, right, number, shift=0):
    lane = (lanes_of(own) + (LANES - shift)) % LANES
    result = jnp.where(lane < 16, turn(right, 12 - 4 * number + shift), 0.0)
    result = jnp.where(lane < 12, own, result)
    return jnp.where(lane < 4, turn(left, shift - 4 * number), result)


def pack_edges(values):
    lane = lanes_of(values[0])
    last = first = jnp.zeros(values[0].shape, jnp.float32)
    for number, value in enumerate(values):
        mine = (lane >= 4 * number) & (lane < 4 * number + 4)
        last = jnp.where(mine, turn(value, 4 * number + 4), last)
        first = jnp.where(mine, turn(value, 4 * number), first)
    return last, first


def kernel(
    nx, ny, rhs, nz, rows, total_cells,
    v_hbm, c_hbm, high, low, out, last_gram, lower_inv, panels, upper,
    v_in, c_in, wide, wide_edge, tile, edge, ghost, packed, landed, packed_c, landed_c,
    packed_edge, ghost_edge, padded, padded_edge, own_edge, own_c, gram_x, gram_y,
    load_sem, halo_send, halo_recv, coef_send, coef_recv, gx_send, gx_recv, gy_send, gy_recv,
):
    gx, gy = lax.axis_index("gx"), lax.axis_index("gy")
    cells = nz * rows
    up, down = lax.rem(gx + 1, nx), lax.rem(gx + nx - 1, nx)
    has_left, has_right = gy > 0, gy < ny - 1
    around = (down, gx, up)
    there = (gy - 1, gy + 1)
    present = (has_left, has_right)

    load_v = pltpu.make_async_copy(v_hbm, v_in, load_sem.at[0])
    load_c = pltpu.make_async_copy(c_hbm, c_in, load_sem.at[1])
    load_v.start()
    load_c.start()

    pair, place = gy // 2, gy % 2
    plane, planes = 2 * gx + place, 2 * nx
    pairs = ny // 2

    def in_plane(i):
        other = lax.rem(plane + i, planes)
        return other, {"gx": other // 2, "gy": 2 * pair + other % 2}

    def in_line(i):
        other = lax.rem(pair + i, pairs)
        return other, {"gx": gx, "gy": 2 * other + place}

    barrier = pltpu.get_barrier_semaphore()

    def greet(device):
        pl.semaphore_signal(barrier, inc=1, device_id=device, device_id_type=MESH)

    across = gy + 2 * place - 1
    has_across = (across >= 0) & (across < ny)

    @pl.when(has_across)
    def _():
        for x in around:
            greet({"gx": x, "gy": across})
    each(1, pairs, lambda i: greet(in_line(i)[1]))
    each(1, planes, lambda i: greet(in_plane(i)[1]))

    lane = lax.broadcasted_iota(jnp.int32, (rhs, LANES), 1)

    for side in SIDES:
        @pl.when(jnp.logical_not(present[side]))
        def _():
            landed[side] = jnp.zeros((3, rhs, LANES), jnp.float32)
            landed_c[side] = jnp.zeros((cells, LANES), jnp.float32)

    lower_inv[...] = jnp.zeros_like(lower_inv)
    panels[...] = jnp.zeros_like(panels)
    upper[...] = jnp.zeros_like(upper)

    def keep(j, number, value):
        at = pl.ds(number * LANES, LANES)
        high[pl.ds(j * rhs, rhs), at], low[pl.ds(j * rhs, rhs), at] = split(value)

    def row_copy(s, side):
        return pltpu.make_async_remote_copy(
            src_ref=tile.at[s, :, rows - 1 if side == 0 else 0],
            dst_ref=ghost.at[s, side],
            send_sem=halo_send.at[s, side],
            recv_sem=halo_recv.at[s, side],
            device_id={"gx": up if side == 0 else down, "gy": gy},
            device_id_type=MESH,
        )

    def column_copy(side, slot):
        return pltpu.make_async_remote_copy(
            src_ref=packed.at[side],
            dst_ref=landed.at[side, slot],
            send_sem=halo_send.at[0, 2 + 3 * side + slot],
            recv_sem=halo_recv.at[0, 2 + 3 * side + slot],
            device_id={"gx": around[2 - slot], "gy": there[1 - side]},
            device_id_type=MESH,
        )

    def coefficient_copy(side):
        return pltpu.make_async_remote_copy(
            src_ref=packed_c.at[side],
            dst_ref=landed_c.at[side],
            send_sem=coef_send.at[side],
            recv_sem=coef_recv.at[side],
            device_id={"gx": gx, "gy": there[1 - side]},
            device_id_type=MESH,
        )

    def edge_copy(s, side):
        return pltpu.make_async_remote_copy(
            src_ref=packed_edge.at[s, side],
            dst_ref=ghost_edge.at[s, side],
            send_sem=halo_send.at[s, 2 + side],
            recv_sem=halo_recv.at[s, 2 + side],
            device_id={"gx": up if side == 0 else down, "gy": gy},
            device_id_type=MESH,
        )

    def send_rows(s):
        for side in SIDES:
            row_copy(s, side).start()

    def send_edges(s):
        lane8 = lax.broadcasted_iota(jnp.int32, (8, LANES), 1)
        for side in SIDES:
            x = rows - 1 if side == 0 else 0
            held = jnp.zeros((8, LANES), jnp.float32)
            for z in range(nz):
                for half in range(rhs // 8):
                    at = 16 * (z * (rhs // 8) + half)
                    value = edge[s, z, x, 8 * half : 8 * half + 8, :]
                    held = jnp.where((lane8 >= at) & (lane8 < at + 16), turn(value, at), held)
            packed_edge[s, side] = held
            edge_copy(s, side).start()

    def ghost_edge_tile(s, side, z):
        if s == 0:
            slot = 2 * side
            number = z * rows + (rows - 1 if side == 0 else 0)
            own = edge_own(ghost[0, side, z])
            return edge_windows(own, landed[0, slot], landed[1, slot], number)
        held = ghost_edge[s, side]
        per = rhs // 8
        parts = [turn(held, -16 * (z * per + half)) for half in range(per)]
        return jnp.concatenate(parts, axis=0)

    def put_ghosts(s):
        for side in SIDES:
            for z in range(nz):
                padded[z, side * (rows + 1)] = ghost[s, side, z]
                padded_edge[z, side * (rows + 1)] = ghost_edge_tile(s, side, z)

    def sums(z, weights, values, wanted):
        parts = {dy: None for dy in wanted}
        for dz in (-1, 0, 1):
            if not 0 <= z + dz < nz:
                continue
            for dx in (-1, 0, 1):
                window = values[z + dz, 1 + dx : 1 + dx + rows]
                window = window.reshape(rows, rhs // 8, 8, LANES)
                for dy in wanted:
                    number = 9 * (dz + 1) + 3 * (dx + 1) + (dy + 1)
                    weight = weights[number, z * rows : (z + 1) * rows]
                    term = weight[:, None] * window
                    parts[dy] = term if parts[dy] is None else parts[dy] + term
        return {dy: part.reshape(rows, rhs, LANES) for dy, part in parts.items()}

    def apply_operator(s):
        more = s + 1 < STEPS
        for z in range(nz):
            near = sums(z, wide_edge, padded_edge, (-1, 0, 1) if more else (-1, 1))
            here = sums(z, wide, padded, (-1, 0, 1))
            for x in range(rows):
                before, after = near[-1][x], near[1][x]
                value = here[0][x]
                value = value + jnp.where(lane == 0, turn(before, -3), turn(here[-1][x], 1))
                value = value + jnp.where(
                    lane == LANES - 1, turn(after, LANES - 13), turn(here[1][x], -1)
                )
                if s > 0:
                    value = 2.0 * value - tile[s - 1, z, x]
                keep(s + 1, z * rows + x, value)
                if more:
                    tile[s + 1, z, x] = value
                    value = near[0][x] + turn(before, 1) + turn(after, -1)
                    if s > 0:
                        value = 2.0 * value - edge[s - 1, z, x]
                    edge[s + 1, z, x] = value

    def fill_padded(s):
        for z in range(nz):
            for x in range(rows):
                padded[z, 1 + x] = tile[s, z, x]
                padded_edge[z, 1 + x] = edge[s, z, x]

    def group_rows(g):
        return pl.ds(GROUPS[g][0] * rhs, (GROUPS[g][1] - GROUPS[g][0]) * rhs)

    def gx_copy(g, slot, other, device):
        part = gram_x.at[slot, group_rows(g)]
        return pltpu.make_async_remote_copy(
            src_ref=part, dst_ref=part,
            send_sem=gx_send.at[g, other], recv_sem=gx_recv.at[g, slot],
            device_id=device, device_id_type=MESH,
        )

    def gy_copy(g, slot, other, device):
        part = gram_y.at[slot, group_rows(g)]
        return pltpu.make_async_remote_copy(
            src_ref=part, dst_ref=part,
            send_sem=gy_send.at[g, other], recv_sem=gy_recv.at[g, slot],
            device_id=device, device_id_type=MESH,
        )

    def local_gram(g):
        at, upto = GROUPS[g][0] * rhs, GROUPS[g][1] * rhs
        part = product((high[at:upto, :], low[at:upto, :]), (high[0:upto, :], low[0:upto, :]), NT)
        gram_x[plane, group_rows(g)] = jnp.concatenate(
            [part, jnp.zeros((upto - at, LANES - upto), jnp.float32)], axis=1
        )
        def go(i):
            gx_copy(g, plane, *in_plane(i)).start()
        each(1, planes, go)

    def gram_over_gx(g):
        def wait(i):
            other, device = in_plane(i)
            gx_copy(g, other, other, device).wait_recv()
        each(1, planes, wait)
        gram_y[pair, group_rows(g)] = jnp.sum(gram_x[:, group_rows(g)], axis=0)
        def go(i):
            gy_copy(g, pair, *in_line(i)).start()
        each(1, pairs, go)

    def wait_gram(g):
        def wait(i):
            other, device = in_line(i)
            gy_copy(g, other, other, device).wait_recv()
        each(1, pairs, wait)

    def gram_block(j):
        return jnp.sum(gram_y[:, j * rhs : (j + 1) * rhs], axis=0) / jnp.float32(total_cells)

    def finish_gram(g):
        def done_x(i):
            gx_copy(g, plane, *in_plane(i)).wait_send()
        each(1, planes, done_x)
        def done_y(i):
            gy_copy(g, pair, *in_line(i)).wait_send()
        each(1, pairs, done_y)

    def factor_block(j):
        at = j * rhs
        here = slice(at, at + rhs)
        panel, inverse, diagonal = factor_rows(
            gram_block(j), lower_inv[...], at, rhs, BLOCKS * rhs
        )
        panels[here, :] = panel
        lower_inv[here, :] = inverse
        upper[here, :] = diagonal

    def apply_block(j):
        at, upto = j * rhs, (j + 1) * rhs
        put_rows(lower_inv[at:upto, 0:upto], high[0:upto, :], low[0:upto, :], out.at[j], cells)

    load_v.wait()
    values = []
    for number in range(cells):
        value = v_in[pl.ds(number, rhs, stride=cells), :]
        tile[0, number // rows, number % rows] = value
        keep(0, number, value)
        values.append(value)
    packed[0], packed[1] = pack_edges(values)

    def weights_of(number):
        return 2.0 * c_in[number * cells : (number + 1) * cells, :] - (3.0 if number == 13 else 0.0)

    load_c.wait()
    packed_c[0], packed_c[1] = pack_edges([weights_of(number) for number in range(27)])
    pl.semaphore_wait(
        barrier, (planes - 1) + (pairs - 1) + 3 * has_across.astype(jnp.int32)
    )
    send_rows(0)
    for side in SIDES:
        @pl.when(present[1 - side])
        def _():
            for slot in range(3):
                column_copy(side, slot).start()
            coefficient_copy(side).start()
    for number in range(27):
        weight = turn(weights_of(number), number % 3 - 1)
        wide[number] = jnp.broadcast_to(weight[:, None, :], (cells, 8, LANES))
        own_c[number] = edge_own(weights_of(number), number % 3 - 1)
    for number in range(cells):
        own_edge[number] = edge_own(tile[0, number // rows, number % rows])

    last = BLOCKS - 1
    for s in range(STEPS):
        if s == 1:
            local_gram(0)
        if s == 2:
            gram_over_gx(0)
        if s == 3:
            local_gram(1)
            wait_gram(0)
            factor_block(0)
        if s > 0:
            fill_padded(s)
        for side in SIDES:
            row_copy(s, side).wait_recv()
            if s > 0:
                edge_copy(s, side).wait_recv()
        if s == 0:
            for side in SIDES:
                @pl.when(present[side])
                def _():
                    coefficient_copy(side).wait_recv()
                    for slot in range(3):
                        column_copy(side, slot).wait_recv()
            for number in range(cells):
                z, x = number // rows, number % rows
                edge[0, z, x] = edge_windows(own_edge[number], landed[0, 1], landed[1, 1], number)
            for number in range(27):
                weight = edge_windows(
                    own_c[number], landed_c[0], landed_c[1], number, number % 3 - 1
                )
                wide_edge[number] = jnp.broadcast_to(weight[:, None, :], (cells, 8, LANES))
            fill_padded(s)
        put_ghosts(s)
        apply_operator(s)
        if s + 1 < STEPS:
            send_rows(s + 1)
            send_edges(s + 1)

    local_gram(2)
    gram_over_gx(1)
    factor_block(1)
    apply_block(0)
    apply_block(1)
    gram_over_gx(2)
    for s in range(STEPS):
        for side in SIDES:
            row_copy(s, side).wait_send()
            if s > 0:
                edge_copy(s, side).wait_send()
    for side in SIDES:
        @pl.when(present[1 - side])
        def _():
            for slot in range(3):
                column_copy(side, slot).wait_send()
            coefficient_copy(side).wait_send()
    finish_gram(0)
    wait_gram(1)
    factor_block(2)
    apply_block(2)
    factor_block(3)
    apply_block(3)
    finish_gram(1)
    wait_gram(2)
    last_gram[...] = gram_block(last)
    finish_gram(2)


def finish_kernel(
    rhs, cells, high, low, first, last_gram, lower_inv, panels, upper, q_hbm, r_hbm,
    out, square, sem,
):
    total, last = BLOCKS * rhs, BLOCKS - 1
    store_first = pltpu.make_async_copy(first, q_hbm.at[pl.ds(0, last), :, :], sem.at[0])
    store_last = pltpu.make_async_copy(out, q_hbm.at[last], sem.at[1])
    store_square = pltpu.make_async_copy(square, r_hbm, sem.at[2])
    store_first.start()
    at = last * rhs
    panel, inverse, diagonal = factor_rows(last_gram[...], lower_inv[...], at, rhs, total)
    put_rows(inverse[:, 0:total], high[...], low[...], out, cells)
    store_last.start()
    pad = jnp.zeros((LANES - total, LANES), jnp.float32)
    lower = jnp.concatenate([panels[0:at, :], panel, pad], axis=0)
    diagonals = jnp.concatenate([upper[0:at, :], diagonal, pad], axis=0)
    square[...] = (jnp.transpose(lower) + diagonals)[0:total, 0:total]
    store_square.start()
    store_first.wait()
    store_last.wait()
    store_square.wait()


def local(nx, ny, right_sides, coefficients):
    rhs, nz, rows, columns = right_sides.shape
    cells = nz * rows
    total = BLOCKS * rhs
    size = rhs * cells
    f32, b16 = jnp.float32, jnp.bfloat16
    vmem = pl.BlockSpec(memory_space=pltpu.VMEM)
    hbm = pl.BlockSpec(memory_space=pltpu.HBM)
    shape = jax.ShapeDtypeStruct
    parts = pl.pallas_call(
        functools.partial(kernel, nx, ny, rhs, nz, rows, nx * ny * cells * columns),
        out_shape=(
            shape((total, cells * LANES), b16),
            shape((total, cells * LANES), b16),
            shape((BLOCKS - 1, size, columns), f32),
            shape((rhs, LANES), f32),
            shape((LANES, LANES), f32),
            shape((total, LANES), f32),
            shape((total, LANES), f32),
        ),
        in_specs=[hbm] * 2,
        out_specs=(vmem,) * 7,
        scratch_shapes=[
            pltpu.VMEM((size, columns), f32),
            pltpu.VMEM((27 * cells, columns), f32),
            pltpu.VMEM((27, cells, 8, LANES), f32),
            pltpu.VMEM((27, cells, 8, LANES), f32),
            pltpu.VMEM((STEPS, nz, rows, rhs, LANES), f32),
            pltpu.VMEM((STEPS, nz, rows, rhs, LANES), f32),
            pltpu.VMEM((STEPS, 2, nz, rhs, LANES), f32),
            pltpu.VMEM((2, rhs, LANES), f32),
            pltpu.VMEM((2, 3, rhs, LANES), f32),
            pltpu.VMEM((2, cells, LANES), f32),
            pltpu.VMEM((2, cells, LANES), f32),
            pltpu.VMEM((STEPS, 2, 8, LANES), f32),
            pltpu.VMEM((STEPS, 2, 8, LANES), f32),
            pltpu.VMEM((nz, rows + 2, rhs, LANES), f32),
            pltpu.VMEM((nz, rows + 2, rhs, LANES), f32),
            pltpu.VMEM((cells, rhs, LANES), f32),
            pltpu.VMEM((27, cells, LANES), f32),
            pltpu.VMEM((2 * nx, total, LANES), f32),
            pltpu.VMEM((ny // 2, total, LANES), f32),
            pltpu.SemaphoreType.DMA((2,)),
            pltpu.SemaphoreType.DMA((STEPS, 8)),
            pltpu.SemaphoreType.DMA((STEPS, 8)),
            pltpu.SemaphoreType.DMA((2,)),
            pltpu.SemaphoreType.DMA((2,)),
            pltpu.SemaphoreType.DMA((len(GROUPS), 2 * nx)),
            pltpu.SemaphoreType.DMA((len(GROUPS), 2 * nx)),
            pltpu.SemaphoreType.DMA((len(GROUPS), ny // 2)),
            pltpu.SemaphoreType.DMA((len(GROUPS), ny // 2)),
        ],
        compiler_params=pltpu.CompilerParams(
            collective_id=0, has_side_effects=True, vmem_limit_bytes=32 * 1024 * 1024
        ),
    )(
        pltpu.with_memory_space_constraint(right_sides.reshape(size, columns), pltpu.HBM),
        pltpu.with_memory_space_constraint(coefficients.reshape(27 * cells, columns), pltpu.HBM),
    )
    solved, square = pl.pallas_call(
        functools.partial(finish_kernel, rhs, cells),
        out_shape=(shape((BLOCKS, size, columns), f32), shape((total, total), f32)),
        in_specs=[vmem] * 7,
        out_specs=(hbm, hbm),
        scratch_shapes=[
            pltpu.VMEM((size, columns), f32),
            pltpu.VMEM((total, total), f32),
            pltpu.SemaphoreType.DMA((3,)),
        ],
        compiler_params=pltpu.CompilerParams(vmem_limit_bytes=16 * 1024 * 1024),
    )(*parts)
    return solved.reshape(total, nz, rows, columns), square


def solution(mesh):
    placed = (P(None, None, "gx", "gy"), P(None, None, "gx", "gy"))
    return jax.shard_map(
        functools.partial(local, mesh.shape["gx"], mesh.shape["gy"]),
        mesh=mesh,
        in_specs=placed,
        out_specs=(P(None, None, "gx", "gy"), P()),
        check_vma=False,
    )
```

```python
import functools

import jax
import jax.numpy as jnp
from jax import lax
from jax.experimental import pallas as pl
from jax.experimental.pallas import tpu as pltpu
from jax.sharding import PartitionSpec as P

MESH = pl.DeviceIdType.MESH
STEPS = 4
BLOCKS = STEPS + 1
LANES = 128
SIDES = (0, 1)
NT = (((1,), (1,)), ((), ()))
NN = (((1,), (0,)), ((), ()))
GROUPS = ((0, 2), (2, 4), (4, 5))


def split(value):
    high = value.astype(jnp.bfloat16)
    return high, (value - high.astype(jnp.float32)).astype(jnp.bfloat16)


def product(a, b, dims):
    rows = a[0].shape[0]
    both = lax.dot_general(
        jnp.concatenate(a, axis=0), b[0], dims, preferred_element_type=jnp.float32
    )
    cross = lax.dot_general(a[0], b[1], dims, preferred_element_type=jnp.float32)
    return both[:rows] + (both[rows:] + cross)


def each(start, stop, body):
    if stop - start <= 8:
        for i in range(start, stop):
            body(i)
    else:
        lax.fori_loop(start, stop, lambda i, c: (body(i), c)[1], 0)


def reciprocal(value):
    guess = pl.reciprocal(value, approx=True)
    guess = guess * (2.0 - value * guess)
    return guess * (2.0 - value * guess)


def inverse_root(value):
    guess = lax.rsqrt(value)
    return guess * (1.5 - 0.5 * value * guess * guess)


def eliminate(work, at, rhs):
    shape = work.shape
    row = lax.broadcasted_iota(jnp.int32, shape, 0)
    scale = jnp.zeros(shape, jnp.float32)
    ratio = jnp.zeros(shape, jnp.float32)
    for k in range(0, rhs, 2):
        col0 = jnp.broadcast_to(work[:, at + k : at + k + 1], shape)
        col1 = jnp.broadcast_to(work[:, at + k + 1 : at + k + 2], shape)
        row0 = jnp.broadcast_to(work[k : k + 1, :], shape)
        row1 = jnp.broadcast_to(work[k + 1 : k + 2, :], shape)
        a = jnp.broadcast_to(col0[k : k + 1, :], shape)
        b = jnp.broadcast_to(col1[k : k + 1, :], shape)
        c = jnp.broadcast_to(col1[k + 1 : k + 2, :], shape)
        over = jnp.where(row > k + 1, reciprocal(a * c - b * b), 0.0)
        slope = b * reciprocal(a)
        ratio = jnp.where(row == k + 1, slope, ratio)
        scale = jnp.where(row == k, inverse_root(a), scale)
        scale = jnp.where(row == k + 1, inverse_root(c - b * slope), scale)
        work = work - ((c * col0 - b * col1) * row0 + (a * col1 - b * col0) * row1) * over
    return (work - ratio * pltpu.roll(work, 1, 0)) * scale


def factor_rows(gram, known, at, rhs, total):
    row = lax.broadcasted_iota(jnp.int32, (rhs, LANES), 0)
    lane = lax.broadcasted_iota(jnp.int32, (rhs, LANES), 1)
    square = pltpu.roll(gram, total - at, 1) if total > at else gram
    unit = jnp.where(lane == at + row, 1.0, 0.0)
    if at:
        known = split(known)
        panel = product(split(gram), known, NT)
        halves = split(panel)
        done = product(halves, halves, NT)
        done = jnp.concatenate([done, jnp.zeros((rhs, LANES - rhs), jnp.float32)], axis=1)
        square = square - pltpu.roll(done, total, 1)
        unit = unit - product(halves, known, NN)
    else:
        panel = jnp.zeros((rhs, LANES), jnp.float32)
    work = eliminate(jnp.where(lane < total, unit, square), total, rhs)
    inverse = jnp.where(lane < total, work, 0.0)
    upper = jnp.where((lane >= total + row) & (lane < total + rhs), work, 0.0)
    return panel, inverse, pltpu.roll(upper, LANES - total + at, 1)


def put_rows(lines, high, low, out, first, rhs, cells):
    solved = product(split(lines), (high, low), NN)
    for block in range(lines.shape[0] // rhs):
        for number in range(cells):
            out[first + block, pl.ds(number, rhs, stride=cells), :] = solved[
                block * rhs : (block + 1) * rhs, number * LANES : (number + 1) * LANES
            ]


def turn(value, shift):
    if isinstance(shift, int):
        shift %= LANES
        return pltpu.roll(value, shift, 1) if shift else value
    return pltpu.roll(value, lax.rem(shift + 8 * LANES, LANES), 1)


def lanes_of(value):
    return lax.broadcasted_iota(jnp.int32, value.shape, 1)


def edge_own(value, shift=0):
    lane = (lanes_of(value) + (LANES - shift)) % LANES
    return jnp.where(lane < 8, turn(value, 4 + shift), turn(value, 12 + shift))


def edge_windows(own, left, right, number, shift=0):
    lane = (lanes_of(own) + (LANES - shift)) % LANES
    result = jnp.where(lane < 16, turn(right, 12 - 4 * number + shift), 0.0)
    result = jnp.where(lane < 12, own, result)
    return jnp.where(lane < 4, turn(left, shift - 4 * number), result)


def pack_edges(count, unroll, get, shape):
    def more(step, held):
        last, first = held
        for part in range(unroll):
            number = step * unroll + part
            value = get(number)
            lane = lanes_of(value)
            mine = (lane >= 4 * number) & (lane < 4 * number + 4)
            last = jnp.where(mine, turn(value, 4 * number + 4), last)
            first = jnp.where(mine, turn(value, 4 * number), first)
        return last, first
    zero = jnp.zeros(shape, jnp.float32)
    return lax.fori_loop(0, count // unroll, more, (zero, zero))


def loop(count, body):
    lax.fori_loop(0, count, lambda i, c: (body(i), c)[1], 0)


def kernel(
    nx, ny, rhs, nz, rows, total_cells,
    v_hbm, c_hbm, high, low, out, last_gram, lower_inv, panels, upper,
    v_in, c_in, wide, wide_edge, tile, edge, ghost, packed, landed, packed_c, landed_c,
    packed_edge, ghost_edge, padded, padded_edge, own_edge, own_c, gram_x, gram_y,
    load_sem, halo_send, halo_recv, coef_send, coef_recv, gx_send, gx_recv, gy_send, gy_recv,
):
    gx, gy = lax.axis_index("gx"), lax.axis_index("gy")
    cells = nz * rows
    up, down = lax.rem(gx + 1, nx), lax.rem(gx + nx - 1, nx)
    has_left, has_right = gy > 0, gy < ny - 1
    around = (down, gx, up)
    there = (gy - 1, gy + 1)
    present = (has_left, has_right)

    load_v = pltpu.make_async_copy(v_hbm, v_in, load_sem.at[0])
    load_c = pltpu.make_async_copy(c_hbm, c_in, load_sem.at[1])
    load_v.start()
    load_c.start()

    pair, place = gy // 2, gy % 2
    plane, planes = 2 * gx + place, 2 * nx
    pairs = ny // 2

    def in_plane(i):
        other = lax.rem(plane + i, planes)
        return other, {"gx": other // 2, "gy": 2 * pair + other % 2}

    def in_line(i):
        other = lax.rem(pair + i, pairs)
        return other, {"gx": gx, "gy": 2 * other + place}

    barrier = pltpu.get_barrier_semaphore()

    def greet(device):
        pl.semaphore_signal(barrier, inc=1, device_id=device, device_id_type=MESH)

    across = gy + 2 * place - 1
    has_across = (across >= 0) & (across < ny)

    @pl.when(has_across)
    def _():
        for x in around:
            greet({"gx": x, "gy": across})
    each(1, pairs, lambda i: greet(in_line(i)[1]))
    each(1, planes, lambda i: greet(in_plane(i)[1]))

    lane = lax.broadcasted_iota(jnp.int32, (rhs, LANES), 1)

    for side in SIDES:
        @pl.when(jnp.logical_not(present[side]))
        def _():
            landed[side] = jnp.zeros((3, rhs, LANES), jnp.float32)
            landed_c[side] = jnp.zeros((cells, LANES), jnp.float32)

    lower_inv[...] = jnp.zeros_like(lower_inv)
    panels[...] = jnp.zeros_like(panels)
    upper[...] = jnp.zeros_like(upper)

    for plane_out in (0, nz + 1):
        padded[plane_out] = jnp.zeros((rows + 2, rhs, LANES), jnp.float32)
        padded_edge[plane_out] = jnp.zeros((rows + 2, rhs, LANES), jnp.float32)

    def keep(j, number, value):
        at = pl.ds(pl.multiple_of(number * LANES, LANES), LANES)
        high[j, :, at], low[j, :, at] = split(value)

    def flat(ref, start, stop):
        return ref[start:stop].reshape((stop - start) * rhs, cells * LANES)

    def row_copy(s, side):
        return pltpu.make_async_remote_copy(
            src_ref=tile.at[s, :, rows - 1 if side == 0 else 0],
            dst_ref=ghost.at[s, side],
            send_sem=halo_send.at[s, side],
            recv_sem=halo_recv.at[s, side],
            device_id={"gx": up if side == 0 else down, "gy": gy},
            device_id_type=MESH,
        )

    def column_copy(side, slot):
        return pltpu.make_async_remote_copy(
            src_ref=packed.at[side],
            dst_ref=landed.at[side, slot],
            send_sem=halo_send.at[0, 2 + 3 * side + slot],
            recv_sem=halo_recv.at[0, 2 + 3 * side + slot],
            device_id={"gx": around[2 - slot], "gy": there[1 - side]},
            device_id_type=MESH,
        )

    def coefficient_copy(side):
        return pltpu.make_async_remote_copy(
            src_ref=packed_c.at[side],
            dst_ref=landed_c.at[side],
            send_sem=coef_send.at[side],
            recv_sem=coef_recv.at[side],
            device_id={"gx": gx, "gy": there[1 - side]},
            device_id_type=MESH,
        )

    def edge_copy(s, side):
        return pltpu.make_async_remote_copy(
            src_ref=packed_edge.at[s, side],
            dst_ref=ghost_edge.at[s, side],
            send_sem=halo_send.at[s, 2 + side],
            recv_sem=halo_recv.at[s, 2 + side],
            device_id={"gx": up if side == 0 else down, "gy": gy},
            device_id_type=MESH,
        )

    def send_rows(s):
        for side in SIDES:
            row_copy(s, side).start()

    def send_edges(s):
        lane8 = lax.broadcasted_iota(jnp.int32, (8, LANES), 1)
        for side in SIDES:
            x = rows - 1 if side == 0 else 0
            held = jnp.zeros((8, LANES), jnp.float32)
            for z in range(nz):
                for half in range(rhs // 8):
                    at = 16 * (z * (rhs // 8) + half)
                    value = edge[s, z, x, 8 * half : 8 * half + 8, :]
                    held = jnp.where((lane8 >= at) & (lane8 < at + 16), turn(value, at), held)
            packed_edge[s, side] = held
            edge_copy(s, side).start()

    def put_ghosts(s):
        for side in SIDES:
            at = side * (rows + 1)
            for z in range(nz):
                padded[z + 1, at] = ghost[s, side, z]

            @pl.when(s == 0)
            def _():
                slot = 2 * side
                def put(z):
                    number = z * rows + (rows - 1 if side == 0 else 0)
                    own = edge_own(ghost[0, side, z])
                    padded_edge[z + 1, at] = edge_windows(
                        own, landed[0, slot], landed[1, slot], number
                    )
                loop(nz, put)

            @pl.when(s > 0)
            def _():
                held = ghost_edge[s, side]
                per = rhs // 8
                for z in range(nz):
                    parts = [turn(held, -16 * (z * per + half)) for half in range(per)]
                    padded_edge[z + 1, at] = jnp.concatenate(parts, axis=0)

    def sums(z, weights, values):
        parts = {}
        for dz in (-1, 0, 1):
            for dx in (-1, 0, 1):
                window = values[z + 1 + dz, 1 + dx : 1 + dx + rows]
                window = window.reshape(rows, rhs // 8, 8, LANES)
                for dy in (-1, 0, 1):
                    number = 9 * (dz + 1) + 3 * (dx + 1) + (dy + 1)
                    term = weights[number, z][:, None] * window
                    parts[dy] = parts[dy] + term if dy in parts else term
        return {dy: part.reshape(rows, rhs, LANES) for dy, part in parts.items()}

    def apply_operator(s):
        factor_now = jnp.where(s > 0, 2.0, 1.0)
        factor_before = jnp.where(s > 0, 1.0, 0.0)
        before_s = jnp.maximum(s - 1, 0)

        def plane_of(z):
            near = sums(z, wide_edge, padded_edge)
            here = sums(z, wide, padded)
            for x in range(rows):
                before, after = near[-1][x], near[1][x]
                value = here[0][x]
                value = value + jnp.where(lane == 0, turn(before, -3), turn(here[-1][x], 1))
                value = value + jnp.where(
                    lane == LANES - 1, turn(after, LANES - 13), turn(here[1][x], -1)
                )
                value = factor_now * value - factor_before * tile[before_s, z, x]
                keep(s + 1, z * rows + x, value)
                tile[s + 1, z, x] = value
                value = near[0][x] + turn(before, 1) + turn(after, -1)
                edge[s + 1, z, x] = factor_now * value - factor_before * edge[before_s, z, x]
        loop(nz, plane_of)

    def fill_padded(s):
        for z in range(nz):
            for x in range(rows):
                padded[z + 1, 1 + x] = tile[s, z, x]
                padded_edge[z + 1, 1 + x] = edge[s, z, x]

    def group_rows(g):
        return pl.ds(GROUPS[g][0] * rhs, (GROUPS[g][1] - GROUPS[g][0]) * rhs)

    def gx_copy(g, slot, other, device):
        part = gram_x.at[slot, group_rows(g)]
        return pltpu.make_async_remote_copy(
            src_ref=part, dst_ref=part,
            send_sem=gx_send.at[g, other], recv_sem=gx_recv.at[g, slot],
            device_id=device, device_id_type=MESH,
        )

    def gy_copy(g, slot, other, device):
        part = gram_y.at[slot, group_rows(g)]
        return pltpu.make_async_remote_copy(
            src_ref=part, dst_ref=part,
            send_sem=gy_send.at[g, other], recv_sem=gy_recv.at[g, slot],
            device_id=device, device_id_type=MESH,
        )

    def local_gram(g):
        at, upto = GROUPS[g][0] * rhs, GROUPS[g][1] * rhs
        first, stop = GROUPS[g]
        part = product(
            (flat(high, first, stop), flat(low, first, stop)),
            (flat(high, 0, stop), flat(low, 0, stop)),
            NT,
        )
        gram_x[plane, group_rows(g)] = jnp.concatenate(
            [part, jnp.zeros((upto - at, LANES - upto), jnp.float32)], axis=1
        )
        def go(i):
            gx_copy(g, plane, *in_plane(i)).start()
        each(1, planes, go)

    def gram_over_gx(g):
        def wait(i):
            other, device = in_plane(i)
            gx_copy(g, other, other, device).wait_recv()
        each(1, planes, wait)
        gram_y[pair, group_rows(g)] = jnp.sum(gram_x[:, group_rows(g)], axis=0)
        def go(i):
            gy_copy(g, pair, *in_line(i)).start()
        each(1, pairs, go)

    def wait_gram(g):
        def wait(i):
            other, device = in_line(i)
            gy_copy(g, other, other, device).wait_recv()
        each(1, pairs, wait)

    def gram_block(j):
        return jnp.sum(gram_y[:, j * rhs : (j + 1) * rhs], axis=0) / jnp.float32(total_cells)

    def finish_gram(g):
        def done_x(i):
            gx_copy(g, plane, *in_plane(i)).wait_send()
        each(1, planes, done_x)
        def done_y(i):
            gy_copy(g, pair, *in_line(i)).wait_send()
        each(1, pairs, done_y)

    def factor_block(j):
        at = j * rhs
        here = slice(at, at + rhs)
        panel, inverse, diagonal = factor_rows(
            gram_block(j), lower_inv[...], at, rhs, BLOCKS * rhs
        )
        panels[here, :] = panel
        lower_inv[here, :] = inverse
        upper[here, :] = diagonal

    def apply_blocks(start, stop):
        lines = lower_inv[start * rhs : stop * rhs, 0 : stop * rhs]
        put_rows(lines, flat(high, 0, stop), flat(low, 0, stop), out, start, rhs, cells)

    load_v.wait()

    def take(number):
        value = v_in[pl.ds(number, rhs, stride=cells), :]
        tile[0, number // rows, number % rows] = value
        keep(0, number, value)
    for number in range(cells):
        take(number)
    packed[0], packed[1] = pack_edges(
        cells, 4, lambda number: tile[0, number // rows, number % rows], (rhs, LANES)
    )

    def weights_of(number):
        values = c_in[pl.ds(pl.multiple_of(number * cells, cells), cells), :]
        return 2.0 * values - jnp.where(number == 13, 3.0, 0.0)

    def widened(value):
        return jnp.broadcast_to(value[:, None, :], (cells, 8, LANES)).reshape(nz, rows, 8, LANES)

    load_c.wait()
    packed_c[0], packed_c[1] = pack_edges(27, 3, weights_of, (cells, LANES))
    pl.semaphore_wait(
        barrier, (planes - 1) + (pairs - 1) + 3 * has_across.astype(jnp.int32)
    )
    send_rows(0)
    for side in SIDES:
        @pl.when(present[1 - side])
        def _():
            for slot in range(3):
                column_copy(side, slot).start()
            coefficient_copy(side).start()

    def prepare(step):
        for part in range(3):
            number = 3 * step + part
            wide[number] = widened(turn(weights_of(number), part - 1))
            own_c[number] = edge_own(weights_of(number), part - 1)
    loop(9, prepare)
    for number in range(cells):
        own_edge[number] = edge_own(tile[0, number // rows, number % rows])

    for side in SIDES:
        @pl.when(present[side])
        def _():
            coefficient_copy(side).wait_recv()
            for slot in range(3):
                column_copy(side, slot).wait_recv()

    def join_edge(step):
        for part in range(4):
            number = 4 * step + part
            edge[0, number // rows, number % rows] = edge_windows(
                own_edge[number], landed[0, 1], landed[1, 1], number
            )
    loop(cells // 4, join_edge)

    def join_weights(step):
        for part in range(3):
            number = 3 * step + part
            wide_edge[number] = widened(
                edge_windows(own_c[number], landed_c[0], landed_c[1], number, part - 1)
            )
    loop(9, join_weights)

    last = BLOCKS - 1

    def step_of(s):
        @pl.when(s == 1)
        def _():
            local_gram(0)
        @pl.when(s == 2)
        def _():
            gram_over_gx(0)
        @pl.when(s == 3)
        def _():
            local_gram(1)
            wait_gram(0)
            factor_block(0)
        fill_padded(s)
        for side in SIDES:
            row_copy(s, side).wait_recv()
            @pl.when(s > 0)
            def _():
                edge_copy(s, side).wait_recv()
        put_ghosts(s)
        apply_operator(s)

        @pl.when(s + 1 < STEPS)
        def _():
            send_rows(s + 1)
            send_edges(s + 1)
    loop(STEPS, step_of)

    local_gram(2)
    gram_over_gx(1)
    factor_block(1)
    apply_blocks(0, 2)
    gram_over_gx(2)
    for s in range(STEPS):
        for side in SIDES:
            row_copy(s, side).wait_send()
            if s > 0:
                edge_copy(s, side).wait_send()
    for side in SIDES:
        @pl.when(present[1 - side])
        def _():
            for slot in range(3):
                column_copy(side, slot).wait_send()
            coefficient_copy(side).wait_send()
    finish_gram(0)
    wait_gram(1)
    factor_block(2)
    factor_block(3)
    apply_blocks(2, 4)
    finish_gram(1)
    wait_gram(2)
    last_gram[...] = gram_block(last)
    finish_gram(2)


def finish_kernel(
    rhs, cells, high, low, first, last_gram, lower_inv, panels, upper, q_hbm, r_hbm,
    out, square, sem,
):
    total, last = BLOCKS * rhs, BLOCKS - 1
    store_first = pltpu.make_async_copy(first, q_hbm.at[pl.ds(0, last), :, :], sem.at[0])
    store_last = pltpu.make_async_copy(out.at[0], q_hbm.at[last], sem.at[1])
    store_square = pltpu.make_async_copy(square, r_hbm, sem.at[2])
    store_first.start()
    at = last * rhs
    panel, inverse, diagonal = factor_rows(last_gram[...], lower_inv[...], at, rhs, total)
    shape = (total, cells * LANES)
    put_rows(inverse[:, 0:total], high[...].reshape(shape), low[...].reshape(shape), out, 0, rhs, cells)
    store_last.start()
    pad = jnp.zeros((LANES - total, LANES), jnp.float32)
    lower = jnp.concatenate([panels[0:at, :], panel, pad], axis=0)
    diagonals = jnp.concatenate([upper[0:at, :], diagonal, pad], axis=0)
    square[...] = (jnp.transpose(lower) + diagonals)[0:total, 0:total]
    store_square.start()
    store_first.wait()
    store_last.wait()
    store_square.wait()


def local(nx, ny, right_sides, coefficients):
    rhs, nz, rows, columns = right_sides.shape
    cells = nz * rows
    total = BLOCKS * rhs
    size = rhs * cells
    f32, b16 = jnp.float32, jnp.bfloat16
    vmem = pl.BlockSpec(memory_space=pltpu.VMEM)
    hbm = pl.BlockSpec(memory_space=pltpu.HBM)
    shape = jax.ShapeDtypeStruct
    parts = pl.pallas_call(
        functools.partial(kernel, nx, ny, rhs, nz, rows, nx * ny * cells * columns),
        out_shape=(
            shape((BLOCKS, rhs, cells * LANES), b16),
            shape((BLOCKS, rhs, cells * LANES), b16),
            shape((BLOCKS - 1, size, columns), f32),
            shape((rhs, LANES), f32),
            shape((LANES, LANES), f32),
            shape((total, LANES), f32),
            shape((total, LANES), f32),
        ),
        in_specs=[hbm] * 2,
        out_specs=(vmem,) * 7,
        scratch_shapes=[
            pltpu.VMEM((size, columns), f32),
            pltpu.VMEM((27 * cells, columns), f32),
            pltpu.VMEM((27, nz, rows, 8, LANES), f32),
            pltpu.VMEM((27, nz, rows, 8, LANES), f32),
            pltpu.VMEM((BLOCKS, nz, rows, rhs, LANES), f32),
            pltpu.VMEM((BLOCKS, nz, rows, rhs, LANES), f32),
            pltpu.VMEM((STEPS, 2, nz, rhs, LANES), f32),
            pltpu.VMEM((2, rhs, LANES), f32),
            pltpu.VMEM((2, 3, rhs, LANES), f32),
            pltpu.VMEM((2, cells, LANES), f32),
            pltpu.VMEM((2, cells, LANES), f32),
            pltpu.VMEM((STEPS, 2, 8, LANES), f32),
            pltpu.VMEM((STEPS, 2, 8, LANES), f32),
            pltpu.VMEM((nz + 2, rows + 2, rhs, LANES), f32),
            pltpu.VMEM((nz + 2, rows + 2, rhs, LANES), f32),
            pltpu.VMEM((cells, rhs, LANES), f32),
            pltpu.VMEM((27, cells, LANES), f32),
            pltpu.VMEM((2 * nx, total, LANES), f32),
            pltpu.VMEM((ny // 2, total, LANES), f32),
            pltpu.SemaphoreType.DMA((2,)),
            pltpu.SemaphoreType.DMA((STEPS, 8)),
            pltpu.SemaphoreType.DMA((STEPS, 8)),
            pltpu.SemaphoreType.DMA((2,)),
            pltpu.SemaphoreType.DMA((2,)),
            pltpu.SemaphoreType.DMA((len(GROUPS), 2 * nx)),
            pltpu.SemaphoreType.DMA((len(GROUPS), 2 * nx)),
            pltpu.SemaphoreType.DMA((len(GROUPS), ny // 2)),
            pltpu.SemaphoreType.DMA((len(GROUPS), ny // 2)),
        ],
        compiler_params=pltpu.CompilerParams(
            collective_id=0, has_side_effects=True, vmem_limit_bytes=32 * 1024 * 1024
        ),
    )(
        pltpu.with_memory_space_constraint(right_sides.reshape(size, columns), pltpu.HBM),
        pltpu.with_memory_space_constraint(coefficients.reshape(27 * cells, columns), pltpu.HBM),
    )
    solved, square = pl.pallas_call(
        functools.partial(finish_kernel, rhs, cells),
        out_shape=(shape((BLOCKS, size, columns), f32), shape((total, total), f32)),
        in_specs=[vmem] * 7,
        out_specs=(hbm, hbm),
        scratch_shapes=[
            pltpu.VMEM((1, size, columns), f32),
            pltpu.VMEM((total, total), f32),
            pltpu.SemaphoreType.DMA((3,)),
        ],
        compiler_params=pltpu.CompilerParams(vmem_limit_bytes=16 * 1024 * 1024),
    )(*parts)
    return solved.reshape(total, nz, rows, columns), square


def solution(mesh):
    placed = (P(None, None, "gx", "gy"), P(None, None, "gx", "gy"))
    return jax.shard_map(
        functools.partial(local, mesh.shape["gx"], mesh.shape["gy"]),
        mesh=mesh,
        in_specs=placed,
        out_specs=(P(None, None, "gx", "gy"), P()),
        check_vma=False,
    )
```

```python
import functools

import jax
import jax.numpy as jnp
from jax import lax
from jax.experimental import pallas as pl
from jax.experimental.pallas import tpu as pltpu
from jax.sharding import PartitionSpec as P

MESH = pl.DeviceIdType.MESH
STEPS = 4
BLOCKS = STEPS + 1
LANES = 128
SIDES = (0, 1)
NT = (((1,), (1,)), ((), ()))
NN = (((1,), (0,)), ((), ()))
GROUPS = ((0, 2), (2, 4), (4, 5))


def split(value):
    high = value.astype(jnp.bfloat16)
    return high, (value - high.astype(jnp.float32)).astype(jnp.bfloat16)


def product(a, b, dims):
    rows = a[0].shape[0]
    both = lax.dot_general(
        jnp.concatenate(a, axis=0), b[0], dims, preferred_element_type=jnp.float32
    )
    cross = lax.dot_general(a[0], b[1], dims, preferred_element_type=jnp.float32)
    return both[:rows] + (both[rows:] + cross)


def each(start, stop, body):
    if stop - start <= 8:
        for i in range(start, stop):
            body(i)
    else:
        lax.fori_loop(start, stop, lambda i, c: (body(i), c)[1], 0)


def reciprocal(value):
    guess = pl.reciprocal(value, approx=True)
    guess = guess * (2.0 - value * guess)
    return guess * (2.0 - value * guess)


def inverse_root(value):
    guess = lax.rsqrt(value)
    return guess * (1.5 - 0.5 * value * guess * guess)


def eliminate(work, at, rhs):
    shape = work.shape
    row = lax.broadcasted_iota(jnp.int32, shape, 0)
    scale = jnp.zeros(shape, jnp.float32)
    ratio = jnp.zeros(shape, jnp.float32)
    for k in range(0, rhs, 2):
        col0 = jnp.broadcast_to(work[:, at + k : at + k + 1], shape)
        col1 = jnp.broadcast_to(work[:, at + k + 1 : at + k + 2], shape)
        row0 = jnp.broadcast_to(work[k : k + 1, :], shape)
        row1 = jnp.broadcast_to(work[k + 1 : k + 2, :], shape)
        a = jnp.broadcast_to(col0[k : k + 1, :], shape)
        b = jnp.broadcast_to(col1[k : k + 1, :], shape)
        c = jnp.broadcast_to(col1[k + 1 : k + 2, :], shape)
        over = jnp.where(row > k + 1, reciprocal(a * c - b * b), 0.0)
        slope = b * reciprocal(a)
        ratio = jnp.where(row == k + 1, slope, ratio)
        scale = jnp.where(row == k, inverse_root(a), scale)
        scale = jnp.where(row == k + 1, inverse_root(c - b * slope), scale)
        work = work - ((c * col0 - b * col1) * row0 + (a * col1 - b * col0) * row1) * over
    return (work - ratio * pltpu.roll(work, 1, 0)) * scale


def factor_rows(gram, known, at, rhs, total):
    row = lax.broadcasted_iota(jnp.int32, (rhs, LANES), 0)
    lane = lax.broadcasted_iota(jnp.int32, (rhs, LANES), 1)
    square = pltpu.roll(gram, total - at, 1) if total > at else gram
    unit = jnp.where(lane == at + row, 1.0, 0.0)
    if at:
        known = split(known)
        panel = product(split(gram), known, NT)
        halves = split(panel)
        done = product(halves, halves, NT)
        done = jnp.concatenate([done, jnp.zeros((rhs, LANES - rhs), jnp.float32)], axis=1)
        square = square - pltpu.roll(done, total, 1)
        unit = unit - product(halves, known, NN)
    else:
        panel = jnp.zeros((rhs, LANES), jnp.float32)
    work = eliminate(jnp.where(lane < total, unit, square), total, rhs)
    inverse = jnp.where(lane < total, work, 0.0)
    upper = jnp.where((lane >= total + row) & (lane < total + rhs), work, 0.0)
    return panel, inverse, pltpu.roll(upper, LANES - total + at, 1)


def put_rows(inverse_rows, high, low, out, cells):
    rhs = inverse_rows.shape[0]
    solved = product(split(inverse_rows), (high, low), NN)
    for number in range(cells):
        out[pl.ds(number, rhs, stride=cells), :] = solved[:, number * LANES : (number + 1) * LANES]


def turn(value, shift):
    shift %= LANES
    return pltpu.roll(value, shift, 1) if shift else value


def lanes_of(value):
    return lax.broadcasted_iota(jnp.int32, value.shape, 1)


def edge_own(value, shift=0):
    lane = (lanes_of(value) + (LANES - shift)) % LANES
    return jnp.where(lane < 8, turn(value, 4 + shift), turn(value, 12 + shift))


def edge_windows(own, left, right, number, shift=0):
    lane = (lanes_of(own) + (LANES - shift)) % LANES
    result = jnp.where(lane < 16, turn(right, 12 - 4 * number + shift), 0.0)
    result = jnp.where(lane < 12, own, result)
    return jnp.where(lane < 4, turn(left, shift - 4 * number), result)


def pack_edges(values):
    lane = lanes_of(values[0])
    last = first = jnp.zeros(values[0].shape, jnp.float32)
    for number, value in enumerate(values):
        mine = (lane >= 4 * number) & (lane < 4 * number + 4)
        last = jnp.where(mine, turn(value, 4 * number + 4), last)
        first = jnp.where(mine, turn(value, 4 * number), first)
    return last, first


def kernel(
    nx, ny, rhs, nz, rows, total_cells,
    v_hbm, c_hbm, high, low, out, last_gram, lower_inv, panels, upper,
    v_in, c_in, wide, wide_edge, tile, edge, ghost, packed, landed, packed_c, landed_c,
    packed_edge, ghost_edge, padded, padded_edge, own_edge, own_c, gram_x, gram_y,
    load_sem, halo_send, halo_recv, coef_send, coef_recv, gx_send, gx_recv, gy_send, gy_recv,
):
    gx, gy = lax.axis_index("gx"), lax.axis_index("gy")
    cells = nz * rows
    up, down = lax.rem(gx + 1, nx), lax.rem(gx + nx - 1, nx)
    has_left, has_right = gy > 0, gy < ny - 1
    around = (down, gx, up)
    there = (gy - 1, gy + 1)
    present = (has_left, has_right)

    load_v = pltpu.make_async_copy(v_hbm, v_in, load_sem.at[0])
    load_c = pltpu.make_async_copy(c_hbm, c_in, load_sem.at[1])
    load_v.start()
    load_c.start()

    pair, place = gy // 2, gy % 2
    plane, planes = 2 * gx + place, 2 * nx
    pairs = ny // 2

    def in_plane(i):
        other = lax.rem(plane + i, planes)
        return other, {"gx": other // 2, "gy": 2 * pair + other % 2}

    def in_line(i):
        other = lax.rem(pair + i, pairs)
        return other, {"gx": gx, "gy": 2 * other + place}

    barrier = pltpu.get_barrier_semaphore()

    def greet(device):
        pl.semaphore_signal(barrier, inc=1, device_id=device, device_id_type=MESH)

    across = gy + 2 * place - 1
    has_across = (across >= 0) & (across < ny)

    @pl.when(has_across)
    def _():
        for x in around:
            greet({"gx": x, "gy": across})
    each(1, pairs, lambda i: greet(in_line(i)[1]))
    each(1, planes, lambda i: greet(in_plane(i)[1]))

    lane = lax.broadcasted_iota(jnp.int32, (rhs, LANES), 1)

    for side in SIDES:
        @pl.when(jnp.logical_not(present[side]))
        def _():
            landed[side] = jnp.zeros((3, rhs, LANES), jnp.float32)
            landed_c[side] = jnp.zeros((cells, LANES), jnp.float32)

    lower_inv[...] = jnp.zeros_like(lower_inv)
    panels[...] = jnp.zeros_like(panels)
    upper[...] = jnp.zeros_like(upper)

    def keep(j, number, value):
        at = pl.ds(number * LANES, LANES)
        high[pl.ds(j * rhs, rhs), at], low[pl.ds(j * rhs, rhs), at] = split(value)

    def row_copy(s, side):
        return pltpu.make_async_remote_copy(
            src_ref=tile.at[s, :, rows - 1 if side == 0 else 0],
            dst_ref=ghost.at[s, side],
            send_sem=halo_send.at[s, side],
            recv_sem=halo_recv.at[s, side],
            device_id={"gx": up if side == 0 else down, "gy": gy},
            device_id_type=MESH,
        )

    def column_copy(side, slot):
        return pltpu.make_async_remote_copy(
            src_ref=packed.at[side],
            dst_ref=landed.at[side, slot],
            send_sem=halo_send.at[0, 2 + 3 * side + slot],
            recv_sem=halo_recv.at[0, 2 + 3 * side + slot],
            device_id={"gx": around[2 - slot], "gy": there[1 - side]},
            device_id_type=MESH,
        )

    def coefficient_copy(side):
        return pltpu.make_async_remote_copy(
            src_ref=packed_c.at[side],
            dst_ref=landed_c.at[side],
            send_sem=coef_send.at[side],
            recv_sem=coef_recv.at[side],
            device_id={"gx": gx, "gy": there[1 - side]},
            device_id_type=MESH,
        )

    def edge_copy(s, side):
        return pltpu.make_async_remote_copy(
            src_ref=packed_edge.at[s, side],
            dst_ref=ghost_edge.at[s, side],
            send_sem=halo_send.at[s, 2 + side],
            recv_sem=halo_recv.at[s, 2 + side],
            device_id={"gx": up if side == 0 else down, "gy": gy},
            device_id_type=MESH,
        )

    def send_rows(s):
        for side in SIDES:
            row_copy(s, side).start()

    def send_edges(s):
        lane8 = lax.broadcasted_iota(jnp.int32, (8, LANES), 1)
        for side in SIDES:
            x = rows - 1 if side == 0 else 0
            held = jnp.zeros((8, LANES), jnp.float32)
            for z in range(nz):
                for half in range(rhs // 8):
                    at = 16 * (z * (rhs // 8) + half)
                    value = turn(edge[s, z, 8 * half : 8 * half + 8, :], at - 16 * (x + 1))
                    held = jnp.where((lane8 >= at) & (lane8 < at + 16), value, held)
            packed_edge[s, side] = held
            edge_copy(s, side).start()

    def ghost_window(s, side, z):
        at = 16 * side * (rows + 1)
        if s == 0:
            slot = 2 * side
            number = z * rows + (rows - 1 if side == 0 else 0)
            own = edge_own(ghost[0, side, z], at)
            return edge_windows(own, landed[0, slot], landed[1, slot], number, at)
        held = ghost_edge[s, side]
        per = rhs // 8
        parts = [turn(held, at - 16 * (z * per + half)) for half in range(per)]
        return jnp.concatenate(parts, axis=0)

    def put_ghosts(s):
        for z in range(nz):
            window = edge[s, z]
            for side in SIDES:
                at = side * (rows + 1)
                padded[z, at] = ghost[s, side, z]
                there_lane = (lane >= 16 * at) & (lane < 16 * at + 16)
                window = jnp.where(there_lane, ghost_window(s, side, z), window)
            padded_edge[z] = window

    def sums(z):
        parts = {}
        for dz in (-1, 0, 1):
            if not 0 <= z + dz < nz:
                continue
            for dx in (-1, 0, 1):
                window = padded[z + dz, 1 + dx : 1 + dx + rows]
                window = window.reshape(rows, rhs // 8, 8, LANES)
                for dy in (-1, 0, 1):
                    number = 9 * (dz + 1) + 3 * (dx + 1) + (dy + 1)
                    weight = wide[number, z * rows : (z + 1) * rows]
                    term = weight[:, None] * window
                    parts[dy] = parts[dy] + term if dy in parts else term
        return {dy: part.reshape(rows, rhs, LANES) for dy, part in parts.items()}

    def edge_sums(z, wanted):
        result = {}
        for dy in wanted:
            total = None
            for dx in (-1, 0, 1):
                part = None
                for dz in (-1, 0, 1):
                    if not 0 <= z + dz < nz:
                        continue
                    number = 9 * (dz + 1) + 3 * (dx + 1) + (dy + 1)
                    term = wide_edge[number, z][None] * padded_edge[z + dz].reshape(
                        rhs // 8, 8, LANES
                    )
                    part = term if part is None else part + term
                part = turn(part.reshape(rhs, LANES), -16 * dx)
                total = part if total is None else total + part
            result[dy] = total
        return result

    def apply_operator(s):
        more = s + 1 < STEPS
        for z in range(nz):
            near = edge_sums(z, (-1, 0, 1) if more else (-1, 1))
            here = sums(z)
            before, after = near[-1], near[1]
            for x in range(rows):
                at = 16 * (x + 1)
                value = here[0][x]
                value = value + jnp.where(
                    lane == 0, turn(before, -3 - at), turn(here[-1][x], 1)
                )
                value = value + jnp.where(
                    lane == LANES - 1, turn(after, LANES - 13 - at), turn(here[1][x], -1)
                )
                if s > 0:
                    value = 2.0 * value - tile[s - 1, z, x]
                keep(s + 1, z * rows + x, value)
                if more:
                    tile[s + 1, z, x] = value
            if more:
                value = near[0] + turn(before, 1) + turn(after, -1)
                if s > 0:
                    value = 2.0 * value - edge[s - 1, z]
                edge[s + 1, z] = value

    def fill_padded(s):
        for z in range(nz):
            for x in range(rows):
                padded[z, 1 + x] = tile[s, z, x]

    def group_rows(g):
        return pl.ds(GROUPS[g][0] * rhs, (GROUPS[g][1] - GROUPS[g][0]) * rhs)

    def gx_copy(g, slot, other, device):
        part = gram_x.at[slot, group_rows(g)]
        return pltpu.make_async_remote_copy(
            src_ref=part, dst_ref=part,
            send_sem=gx_send.at[g, other], recv_sem=gx_recv.at[g, slot],
            device_id=device, device_id_type=MESH,
        )

    def gy_copy(g, slot, other, device):
        part = gram_y.at[slot, group_rows(g)]
        return pltpu.make_async_remote_copy(
            src_ref=part, dst_ref=part,
            send_sem=gy_send.at[g, other], recv_sem=gy_recv.at[g, slot],
            device_id=device, device_id_type=MESH,
        )

    def local_gram(g):
        at, upto = GROUPS[g][0] * rhs, GROUPS[g][1] * rhs
        part = product((high[at:upto, :], low[at:upto, :]), (high[0:upto, :], low[0:upto, :]), NT)
        gram_x[plane, group_rows(g)] = jnp.concatenate(
            [part, jnp.zeros((upto - at, LANES - upto), jnp.float32)], axis=1
        )
        def go(i):
            gx_copy(g, plane, *in_plane(i)).start()
        each(1, planes, go)

    def gram_over_gx(g):
        def wait(i):
            other, device = in_plane(i)
            gx_copy(g, other, other, device).wait_recv()
        each(1, planes, wait)
        gram_y[pair, group_rows(g)] = jnp.sum(gram_x[:, group_rows(g)], axis=0)
        def go(i):
            gy_copy(g, pair, *in_line(i)).start()
        each(1, pairs, go)

    def wait_gram(g):
        def wait(i):
            other, device = in_line(i)
            gy_copy(g, other, other, device).wait_recv()
        each(1, pairs, wait)

    def gram_block(j):
        return jnp.sum(gram_y[:, j * rhs : (j + 1) * rhs], axis=0) / jnp.float32(total_cells)

    def finish_gram(g):
        def done_x(i):
            gx_copy(g, plane, *in_plane(i)).wait_send()
        each(1, planes, done_x)
        def done_y(i):
            gy_copy(g, pair, *in_line(i)).wait_send()
        each(1, pairs, done_y)

    def factor_block(j):
        at = j * rhs
        here = slice(at, at + rhs)
        panel, inverse, diagonal = factor_rows(
            gram_block(j), lower_inv[...], at, rhs, BLOCKS * rhs
        )
        panels[here, :] = panel
        lower_inv[here, :] = inverse
        upper[here, :] = diagonal

    def apply_block(j):
        at, upto = j * rhs, (j + 1) * rhs
        put_rows(lower_inv[at:upto, 0:upto], high[0:upto, :], low[0:upto, :], out.at[j], cells)

    load_v.wait()
    values = []
    for number in range(cells):
        value = v_in[pl.ds(number, rhs, stride=cells), :]
        tile[0, number // rows, number % rows] = value
        keep(0, number, value)
        values.append(value)
    packed[0], packed[1] = pack_edges(values)

    def weights_of(number):
        return 2.0 * c_in[number * cells : (number + 1) * cells, :] - (3.0 if number == 13 else 0.0)

    load_c.wait()
    packed_c[0], packed_c[1] = pack_edges([weights_of(number) for number in range(27)])
    pl.semaphore_wait(
        barrier, (planes - 1) + (pairs - 1) + 3 * has_across.astype(jnp.int32)
    )
    send_rows(0)
    for side in SIDES:
        @pl.when(present[1 - side])
        def _():
            for slot in range(3):
                column_copy(side, slot).start()
            coefficient_copy(side).start()
    for number in range(27):
        weight = turn(weights_of(number), number % 3 - 1)
        wide[number] = jnp.broadcast_to(weight[:, None, :], (cells, 8, LANES))
        own_c[number] = edge_own(weights_of(number))
    for number in range(cells):
        z, x = number // rows, number % rows
        own_edge[number] = edge_own(tile[0, z, x], 16 * (x + 1))

    last = BLOCKS - 1
    for s in range(STEPS):
        if s == 1:
            local_gram(0)
        if s == 2:
            gram_over_gx(0)
        if s == 3:
            local_gram(1)
            wait_gram(0)
            factor_block(0)
        if s > 0:
            fill_padded(s)
        for side in SIDES:
            row_copy(s, side).wait_recv()
            if s > 0:
                edge_copy(s, side).wait_recv()
        if s == 0:
            for side in SIDES:
                @pl.when(present[side])
                def _():
                    coefficient_copy(side).wait_recv()
                    for slot in range(3):
                        column_copy(side, slot).wait_recv()
            for z in range(nz):
                total = jnp.zeros((rhs, LANES), jnp.float32)
                for x in range(rows):
                    number, at = z * rows + x, 16 * (x + 1)
                    total = total + edge_windows(
                        own_edge[number], landed[0, 1], landed[1, 1], number, at
                    )
                edge[0, z] = total
            place_x = lax.broadcasted_iota(jnp.int32, (cells, LANES), 0) % rows
            for number in range(27):
                dx, dy = number // 3 % 3 - 1, number % 3 - 1
                weight = edge_windows(own_c[number], landed_c[0], landed_c[1], number)
                spread = jnp.zeros((cells, LANES), jnp.float32)
                for x in range(rows):
                    moved = turn(weight, 16 * (x + 1 + dx) + dy)
                    spread = jnp.where(place_x == x, moved, spread)
                for z in range(nz):
                    line = spread[z * rows : z * rows + 1]
                    for x in range(1, rows):
                        line = line + spread[z * rows + x : z * rows + x + 1]
                    wide_edge[number, z] = jnp.broadcast_to(line, (8, LANES))
            fill_padded(s)
        put_ghosts(s)
        apply_operator(s)
        if s + 1 < STEPS:
            send_rows(s + 1)
            send_edges(s + 1)

    local_gram(2)
    gram_over_gx(1)
    factor_block(1)
    apply_block(0)
    apply_block(1)
    gram_over_gx(2)
    for s in range(STEPS):
        for side in SIDES:
            row_copy(s, side).wait_send()
            if s > 0:
                edge_copy(s, side).wait_send()
    for side in SIDES:
        @pl.when(present[1 - side])
        def _():
            for slot in range(3):
                column_copy(side, slot).wait_send()
            coefficient_copy(side).wait_send()
    finish_gram(0)
    wait_gram(1)
    factor_block(2)
    apply_block(2)
    factor_block(3)
    apply_block(3)
    finish_gram(1)
    wait_gram(2)
    last_gram[...] = gram_block(last)
    finish_gram(2)


def finish_kernel(
    rhs, cells, high, low, first, last_gram, lower_inv, panels, upper, q_hbm, r_hbm,
    out, square, sem,
):
    total, last = BLOCKS * rhs, BLOCKS - 1
    store_first = pltpu.make_async_copy(first, q_hbm.at[pl.ds(0, last), :, :], sem.at[0])
    store_last = pltpu.make_async_copy(out, q_hbm.at[last], sem.at[1])
    store_square = pltpu.make_async_copy(square, r_hbm, sem.at[2])
    store_first.start()
    at = last * rhs
    panel, inverse, diagonal = factor_rows(last_gram[...], lower_inv[...], at, rhs, total)
    put_rows(inverse[:, 0:total], high[...], low[...], out, cells)
    store_last.start()
    pad = jnp.zeros((LANES - total, LANES), jnp.float32)
    lower = jnp.concatenate([panels[0:at, :], panel, pad], axis=0)
    diagonals = jnp.concatenate([upper[0:at, :], diagonal, pad], axis=0)
    square[...] = (jnp.transpose(lower) + diagonals)[0:total, 0:total]
    store_square.start()
    store_first.wait()
    store_last.wait()
    store_square.wait()


def local(nx, ny, right_sides, coefficients):
    rhs, nz, rows, columns = right_sides.shape
    cells = nz * rows
    total = BLOCKS * rhs
    size = rhs * cells
    f32, b16 = jnp.float32, jnp.bfloat16
    vmem = pl.BlockSpec(memory_space=pltpu.VMEM)
    hbm = pl.BlockSpec(memory_space=pltpu.HBM)
    shape = jax.ShapeDtypeStruct
    parts = pl.pallas_call(
        functools.partial(kernel, nx, ny, rhs, nz, rows, nx * ny * cells * columns),
        out_shape=(
            shape((total, cells * LANES), b16),
            shape((total, cells * LANES), b16),
            shape((BLOCKS - 1, size, columns), f32),
            shape((rhs, LANES), f32),
            shape((LANES, LANES), f32),
            shape((total, LANES), f32),
            shape((total, LANES), f32),
        ),
        in_specs=[hbm] * 2,
        out_specs=(vmem,) * 7,
        scratch_shapes=[
            pltpu.VMEM((size, columns), f32),
            pltpu.VMEM((27 * cells, columns), f32),
            pltpu.VMEM((27, cells, 8, LANES), f32),
            pltpu.VMEM((27, nz, 8, LANES), f32),
            pltpu.VMEM((STEPS, nz, rows, rhs, LANES), f32),
            pltpu.VMEM((STEPS, nz, rhs, LANES), f32),
            pltpu.VMEM((STEPS, 2, nz, rhs, LANES), f32),
            pltpu.VMEM((2, rhs, LANES), f32),
            pltpu.VMEM((2, 3, rhs, LANES), f32),
            pltpu.VMEM((2, cells, LANES), f32),
            pltpu.VMEM((2, cells, LANES), f32),
            pltpu.VMEM((STEPS, 2, 8, LANES), f32),
            pltpu.VMEM((STEPS, 2, 8, LANES), f32),
            pltpu.VMEM((nz, rows + 2, rhs, LANES), f32),
            pltpu.VMEM((nz, rhs, LANES), f32),
            pltpu.VMEM((cells, rhs, LANES), f32),
            pltpu.VMEM((27, cells, LANES), f32),
            pltpu.VMEM((2 * nx, total, LANES), f32),
            pltpu.VMEM((ny // 2, total, LANES), f32),
            pltpu.SemaphoreType.DMA((2,)),
            pltpu.SemaphoreType.DMA((STEPS, 8)),
            pltpu.SemaphoreType.DMA((STEPS, 8)),
            pltpu.SemaphoreType.DMA((2,)),
            pltpu.SemaphoreType.DMA((2,)),
            pltpu.SemaphoreType.DMA((len(GROUPS), 2 * nx)),
            pltpu.SemaphoreType.DMA((len(GROUPS), 2 * nx)),
            pltpu.SemaphoreType.DMA((len(GROUPS), ny // 2)),
            pltpu.SemaphoreType.DMA((len(GROUPS), ny // 2)),
        ],
        compiler_params=pltpu.CompilerParams(
            collective_id=0, has_side_effects=True, vmem_limit_bytes=32 * 1024 * 1024
        ),
    )(
        pltpu.with_memory_space_constraint(right_sides.reshape(size, columns), pltpu.HBM),
        pltpu.with_memory_space_constraint(coefficients.reshape(27 * cells, columns), pltpu.HBM),
    )
    solved, square = pl.pallas_call(
        functools.partial(finish_kernel, rhs, cells),
        out_shape=(shape((BLOCKS, size, columns), f32), shape((total, total), f32)),
        in_specs=[vmem] * 7,
        out_specs=(hbm, hbm),
        scratch_shapes=[
            pltpu.VMEM((size, columns), f32),
            pltpu.VMEM((total, total), f32),
            pltpu.SemaphoreType.DMA((3,)),
        ],
        compiler_params=pltpu.CompilerParams(vmem_limit_bytes=16 * 1024 * 1024),
    )(*parts)
    return solved.reshape(total, nz, rows, columns), square


def solution(mesh):
    placed = (P(None, None, "gx", "gy"), P(None, None, "gx", "gy"))
    return jax.shard_map(
        functools.partial(local, mesh.shape["gx"], mesh.shape["gy"]),
        mesh=mesh,
        in_specs=placed,
        out_specs=(P(None, None, "gx", "gy"), P()),
        check_vma=False,
    )
```

```python
import functools

import jax
import jax.numpy as jnp
from jax import lax
from jax.experimental import pallas as pl
from jax.experimental.pallas import tpu as pltpu
from jax.sharding import PartitionSpec as P

MESH = pl.DeviceIdType.MESH
STEPS = 4
BLOCKS = STEPS + 1
LANES = 128
SIDES = (0, 1)
NT = (((1,), (1,)), ((), ()))
NN = (((1,), (0,)), ((), ()))
GROUPS = ((0, 1), (1, 3), (3, 4), (4, 5))


def split(value):
    high = value.astype(jnp.bfloat16)
    return high, (value - high.astype(jnp.float32)).astype(jnp.bfloat16)


def product(a, b, dims):
    rows = a[0].shape[0]
    both = lax.dot_general(
        jnp.concatenate(a, axis=0), b[0], dims, preferred_element_type=jnp.float32
    )
    cross = lax.dot_general(a[0], b[1], dims, preferred_element_type=jnp.float32)
    return both[:rows] + (both[rows:] + cross)


def each(start, stop, body):
    if stop - start <= 8:
        for i in range(start, stop):
            body(i)
    else:
        lax.fori_loop(start, stop, lambda i, c: (body(i), c)[1], 0)


def reciprocal(value):
    guess = pl.reciprocal(value, approx=True)
    guess = guess * (2.0 - value * guess)
    return guess * (2.0 - value * guess)


def inverse_root(value):
    guess = lax.rsqrt(value)
    return guess * (1.5 - 0.5 * value * guess * guess)


def eliminate(work, at, rhs):
    shape = work.shape
    row = lax.broadcasted_iota(jnp.int32, shape, 0)
    scale = jnp.zeros(shape, jnp.float32)
    ratio = jnp.zeros(shape, jnp.float32)
    for k in range(0, rhs, 2):
        col0 = jnp.broadcast_to(work[:, at + k : at + k + 1], shape)
        col1 = jnp.broadcast_to(work[:, at + k + 1 : at + k + 2], shape)
        row0 = jnp.broadcast_to(work[k : k + 1, :], shape)
        row1 = jnp.broadcast_to(work[k + 1 : k + 2, :], shape)
        a = jnp.broadcast_to(col0[k : k + 1, :], shape)
        b = jnp.broadcast_to(col1[k : k + 1, :], shape)
        c = jnp.broadcast_to(col1[k + 1 : k + 2, :], shape)
        over = jnp.where(row > k + 1, reciprocal(a * c - b * b), 0.0)
        slope = b * reciprocal(a)
        ratio = jnp.where(row == k + 1, slope, ratio)
        scale = jnp.where(row == k, inverse_root(a), scale)
        scale = jnp.where(row == k + 1, inverse_root(c - b * slope), scale)
        work = work - ((c * col0 - b * col1) * row0 + (a * col1 - b * col0) * row1) * over
    return (work - ratio * pltpu.roll(work, 1, 0)) * scale


def factor_rows(gram, known, at, rhs, total):
    row = lax.broadcasted_iota(jnp.int32, (rhs, LANES), 0)
    lane = lax.broadcasted_iota(jnp.int32, (rhs, LANES), 1)
    square = pltpu.roll(gram, total - at, 1) if total > at else gram
    unit = jnp.where(lane == at + row, 1.0, 0.0)
    if at:
        known = split(known)
        panel = product(split(gram), known, NT)
        halves = split(panel)
        done = product(halves, halves, NT)
        done = jnp.concatenate([done, jnp.zeros((rhs, LANES - rhs), jnp.float32)], axis=1)
        square = square - pltpu.roll(done, total, 1)
        unit = unit - product(halves, known, NN)
    else:
        panel = jnp.zeros((rhs, LANES), jnp.float32)
    work = eliminate(jnp.where(lane < total, unit, square), total, rhs)
    inverse = jnp.where(lane < total, work, 0.0)
    upper = jnp.where((lane >= total + row) & (lane < total + rhs), work, 0.0)
    return panel, inverse, pltpu.roll(upper, LANES - total + at, 1)


def put_rows(inverse_rows, high, low, out, cells):
    rhs = inverse_rows.shape[0]
    solved = product(split(inverse_rows), (high, low), NN)
    for number in range(cells):
        out[pl.ds(number, rhs, stride=cells), :] = solved[:, number * LANES : (number + 1) * LANES]


def turn(value, shift):
    shift %= LANES
    return pltpu.roll(value, shift, 1) if shift else value


def lanes_of(value):
    return lax.broadcasted_iota(jnp.int32, value.shape, 1)


def edge_own(value, shift=0):
    lane = (lanes_of(value) + (LANES - shift)) % LANES
    return jnp.where(lane < 8, turn(value, 4 + shift), turn(value, 12 + shift))


def edge_windows(own, left, right, number, shift=0):
    lane = (lanes_of(own) + (LANES - shift)) % LANES
    result = jnp.where(lane < 16, turn(right, 12 - 4 * number + shift), 0.0)
    result = jnp.where(lane < 12, own, result)
    return jnp.where(lane < 4, turn(left, shift - 4 * number), result)


def pack_edges(values):
    lane = lanes_of(values[0])
    last = first = jnp.zeros(values[0].shape, jnp.float32)
    for number, value in enumerate(values):
        mine = (lane >= 4 * number) & (lane < 4 * number + 4)
        last = jnp.where(mine, turn(value, 4 * number + 4), last)
        first = jnp.where(mine, turn(value, 4 * number), first)
    return last, first


def kernel(
    nx, ny, rhs, nz, rows, total_cells,
    v_hbm, c_hbm, high, low, out, last_gram, lower_inv, panels, upper,
    v_in, c_in, wide, wide_edge, tile, edge, ghost, packed, landed, packed_c, landed_c,
    packed_edge, ghost_edge, padded, padded_edge, own_edge, own_c, gram_x, gram_y,
    load_sem, halo_send, halo_recv, coef_send, coef_recv, gx_send, gx_recv, gy_send, gy_recv,
):
    gx, gy = lax.axis_index("gx"), lax.axis_index("gy")
    cells = nz * rows
    up, down = lax.rem(gx + 1, nx), lax.rem(gx + nx - 1, nx)
    has_left, has_right = gy > 0, gy < ny - 1
    around = (down, gx, up)
    there = (gy - 1, gy + 1)
    present = (has_left, has_right)

    load_v = pltpu.make_async_copy(v_hbm, v_in, load_sem.at[0])
    load_c = pltpu.make_async_copy(c_hbm, c_in, load_sem.at[1])
    load_v.start()
    load_c.start()

    pair, place = gy // 2, gy % 2
    plane, planes = 2 * gx + place, 2 * nx
    pairs = ny // 2

    def in_plane(i):
        other = lax.rem(plane + i, planes)
        return other, {"gx": other // 2, "gy": 2 * pair + other % 2}

    def in_line(i):
        other = lax.rem(pair + i, pairs)
        return other, {"gx": gx, "gy": 2 * other + place}

    barrier = pltpu.get_barrier_semaphore()

    def greet(device):
        pl.semaphore_signal(barrier, inc=1, device_id=device, device_id_type=MESH)

    across = gy + 2 * place - 1
    has_across = (across >= 0) & (across < ny)

    @pl.when(has_across)
    def _():
        for x in around:
            greet({"gx": x, "gy": across})
    each(1, pairs, lambda i: greet(in_line(i)[1]))
    each(1, planes, lambda i: greet(in_plane(i)[1]))

    lane = lax.broadcasted_iota(jnp.int32, (rhs, LANES), 1)

    for side in SIDES:
        @pl.when(jnp.logical_not(present[side]))
        def _():
            landed[side] = jnp.zeros((3, rhs, LANES), jnp.float32)
            landed_c[side] = jnp.zeros((cells, LANES), jnp.float32)

    lower_inv[...] = jnp.zeros_like(lower_inv)
    panels[...] = jnp.zeros_like(panels)
    upper[...] = jnp.zeros_like(upper)

    def keep(j, number, value):
        at = pl.ds(number * LANES, LANES)
        high[pl.ds(j * rhs, rhs), at], low[pl.ds(j * rhs, rhs), at] = split(value)

    def row_copy(s, side):
        return pltpu.make_async_remote_copy(
            src_ref=tile.at[s, :, rows - 1 if side == 0 else 0],
            dst_ref=ghost.at[s, side],
            send_sem=halo_send.at[s, side],
            recv_sem=halo_recv.at[s, side],
            device_id={"gx": up if side == 0 else down, "gy": gy},
            device_id_type=MESH,
        )

    def column_copy(side, slot):
        return pltpu.make_async_remote_copy(
            src_ref=packed.at[side],
            dst_ref=landed.at[side, slot],
            send_sem=halo_send.at[0, 2 + 3 * side + slot],
            recv_sem=halo_recv.at[0, 2 + 3 * side + slot],
            device_id={"gx": around[2 - slot], "gy": there[1 - side]},
            device_id_type=MESH,
        )

    def coefficient_copy(side):
        return pltpu.make_async_remote_copy(
            src_ref=packed_c.at[side],
            dst_ref=landed_c.at[side],
            send_sem=coef_send.at[side],
            recv_sem=coef_recv.at[side],
            device_id={"gx": gx, "gy": there[1 - side]},
            device_id_type=MESH,
        )

    def edge_copy(s, side):
        return pltpu.make_async_remote_copy(
            src_ref=packed_edge.at[s, side],
            dst_ref=ghost_edge.at[s, side],
            send_sem=halo_send.at[s, 2 + side],
            recv_sem=halo_recv.at[s, 2 + side],
            device_id={"gx": up if side == 0 else down, "gy": gy},
            device_id_type=MESH,
        )

    def send_rows(s):
        for side in SIDES:
            row_copy(s, side).start()

    def send_edges(s):
        lane8 = lax.broadcasted_iota(jnp.int32, (8, LANES), 1)
        for side in SIDES:
            x = rows - 1 if side == 0 else 0
            held = jnp.zeros((8, LANES), jnp.float32)
            for z in range(nz):
                for half in range(rhs // 8):
                    at = 16 * (z * (rhs // 8) + half)
                    value = turn(edge[s, z, 8 * half : 8 * half + 8, :], at - 16 * (x + 1))
                    held = jnp.where((lane8 >= at) & (lane8 < at + 16), value, held)
            packed_edge[s, side] = held
            edge_copy(s, side).start()

    def ghost_window(s, side, z):
        at = 16 * side * (rows + 1)
        if s == 0:
            slot = 2 * side
            number = z * rows + (rows - 1 if side == 0 else 0)
            own = edge_own(ghost[0, side, z], at)
            return edge_windows(own, landed[0, slot], landed[1, slot], number, at)
        held = ghost_edge[s, side]
        per = rhs // 8
        parts = [turn(held, at - 16 * (z * per + half)) for half in range(per)]
        return jnp.concatenate(parts, axis=0)

    def put_ghosts(s):
        for z in range(nz):
            window = edge[s, z]
            for side in SIDES:
                at = side * (rows + 1)
                padded[z, at] = ghost[s, side, z]
                there_lane = (lane >= 16 * at) & (lane < 16 * at + 16)
                window = jnp.where(there_lane, ghost_window(s, side, z), window)
            padded_edge[z] = window

    def sums(z):
        parts = {}
        for dz in (-1, 0, 1):
            if not 0 <= z + dz < nz:
                continue
            for dx in (-1, 0, 1):
                window = padded[z + dz, 1 + dx : 1 + dx + rows]
                window = window.reshape(rows, rhs // 8, 8, LANES)
                for dy in (-1, 0, 1):
                    number = 9 * (dz + 1) + 3 * (dx + 1) + (dy + 1)
                    weight = wide[number, z * rows : (z + 1) * rows]
                    term = weight[:, None] * window
                    parts[dy] = parts[dy] + term if dy in parts else term
        return {dy: part.reshape(rows, rhs, LANES) for dy, part in parts.items()}

    def edge_sums(z, wanted):
        result = {}
        for dy in wanted:
            total = None
            for dx in (-1, 0, 1):
                part = None
                for dz in (-1, 0, 1):
                    if not 0 <= z + dz < nz:
                        continue
                    number = 9 * (dz + 1) + 3 * (dx + 1) + (dy + 1)
                    term = wide_edge[number, z][None] * padded_edge[z + dz].reshape(
                        rhs // 8, 8, LANES
                    )
                    part = term if part is None else part + term
                part = turn(part.reshape(rhs, LANES), -16 * dx)
                total = part if total is None else total + part
            result[dy] = total
        return result

    def apply_operator(s):
        more = s + 1 < STEPS
        for z in range(nz):
            near = edge_sums(z, (-1, 0, 1) if more else (-1, 1))
            here = sums(z)
            before, after = near[-1], near[1]
            for x in range(rows):
                at = 16 * (x + 1)
                value = here[0][x]
                value = value + jnp.where(
                    lane == 0, turn(before, -3 - at), turn(here[-1][x], 1)
                )
                value = value + jnp.where(
                    lane == LANES - 1, turn(after, LANES - 13 - at), turn(here[1][x], -1)
                )
                if s > 0:
                    value = 2.0 * value - tile[s - 1, z, x]
                keep(s + 1, z * rows + x, value)
                if more:
                    tile[s + 1, z, x] = value
            if more:
                value = near[0] + turn(before, 1) + turn(after, -1)
                if s > 0:
                    value = 2.0 * value - edge[s - 1, z]
                edge[s + 1, z] = value

    def fill_padded(s):
        for z in range(nz):
            for x in range(rows):
                padded[z, 1 + x] = tile[s, z, x]

    def group_rows(g):
        return pl.ds(GROUPS[g][0] * rhs, (GROUPS[g][1] - GROUPS[g][0]) * rhs)

    def gx_copy(g, slot, other, device):
        part = gram_x.at[slot, group_rows(g)]
        return pltpu.make_async_remote_copy(
            src_ref=part, dst_ref=part,
            send_sem=gx_send.at[g, other], recv_sem=gx_recv.at[g, slot],
            device_id=device, device_id_type=MESH,
        )

    def gy_copy(g, slot, other, device):
        part = gram_y.at[slot, group_rows(g)]
        return pltpu.make_async_remote_copy(
            src_ref=part, dst_ref=part,
            send_sem=gy_send.at[g, other], recv_sem=gy_recv.at[g, slot],
            device_id=device, device_id_type=MESH,
        )

    def local_gram(g):
        at, upto = GROUPS[g][0] * rhs, GROUPS[g][1] * rhs
        part = product((high[at:upto, :], low[at:upto, :]), (high[0:upto, :], low[0:upto, :]), NT)
        gram_x[plane, group_rows(g)] = jnp.concatenate(
            [part, jnp.zeros((upto - at, LANES - upto), jnp.float32)], axis=1
        )
        def go(i):
            gx_copy(g, plane, *in_plane(i)).start()
        each(1, planes, go)

    def gram_over_gx(g):
        def wait(i):
            other, device = in_plane(i)
            gx_copy(g, other, other, device).wait_recv()
        each(1, planes, wait)
        gram_y[pair, group_rows(g)] = jnp.sum(gram_x[:, group_rows(g)], axis=0)
        def go(i):
            gy_copy(g, pair, *in_line(i)).start()
        each(1, pairs, go)

    def wait_gram(g):
        def wait(i):
            other, device = in_line(i)
            gy_copy(g, other, other, device).wait_recv()
        each(1, pairs, wait)

    def gram_block(j):
        return jnp.sum(gram_y[:, j * rhs : (j + 1) * rhs], axis=0) / jnp.float32(total_cells)

    def finish_gram(g):
        def done_x(i):
            gx_copy(g, plane, *in_plane(i)).wait_send()
        each(1, planes, done_x)
        def done_y(i):
            gy_copy(g, pair, *in_line(i)).wait_send()
        each(1, pairs, done_y)

    def factor_block(j):
        at = j * rhs
        here = slice(at, at + rhs)
        panel, inverse, diagonal = factor_rows(
            gram_block(j), lower_inv[...], at, rhs, BLOCKS * rhs
        )
        panels[here, :] = panel
        lower_inv[here, :] = inverse
        upper[here, :] = diagonal

    def apply_block(j):
        at, upto = j * rhs, (j + 1) * rhs
        put_rows(lower_inv[at:upto, 0:upto], high[0:upto, :], low[0:upto, :], out.at[j], cells)

    load_v.wait()
    values = []
    for number in range(cells):
        value = v_in[pl.ds(number, rhs, stride=cells), :]
        tile[0, number // rows, number % rows] = value
        keep(0, number, value)
        values.append(value)
    packed[0], packed[1] = pack_edges(values)

    def weights_of(number):
        return 2.0 * c_in[number * cells : (number + 1) * cells, :] - (3.0 if number == 13 else 0.0)

    load_c.wait()
    packed_c[0], packed_c[1] = pack_edges([weights_of(number) for number in range(27)])
    pl.semaphore_wait(
        barrier, (planes - 1) + (pairs - 1) + 3 * has_across.astype(jnp.int32)
    )
    send_rows(0)
    for side in SIDES:
        @pl.when(present[1 - side])
        def _():
            for slot in range(3):
                column_copy(side, slot).start()
            coefficient_copy(side).start()
    for number in range(27):
        weight = turn(weights_of(number), number % 3 - 1)
        wide[number] = jnp.broadcast_to(weight[:, None, :], (cells, 8, LANES))
        own_c[number] = edge_own(weights_of(number))
    for number in range(cells):
        z, x = number // rows, number % rows
        own_edge[number] = edge_own(tile[0, z, x], 16 * (x + 1))

    last = BLOCKS - 1
    for s in range(STEPS):
        if s == 0:
            local_gram(0)
        if s == 1:
            gram_over_gx(0)
        if s == 2:
            local_gram(1)
            wait_gram(0)
            factor_block(0)
        if s == 3:
            local_gram(2)
            gram_over_gx(1)
        if s > 0:
            fill_padded(s)
        for side in SIDES:
            row_copy(s, side).wait_recv()
            if s > 0:
                edge_copy(s, side).wait_recv()
        if s == 0:
            for side in SIDES:
                @pl.when(present[side])
                def _():
                    coefficient_copy(side).wait_recv()
                    for slot in range(3):
                        column_copy(side, slot).wait_recv()
            for z in range(nz):
                total = jnp.zeros((rhs, LANES), jnp.float32)
                for x in range(rows):
                    number, at = z * rows + x, 16 * (x + 1)
                    total = total + edge_windows(
                        own_edge[number], landed[0, 1], landed[1, 1], number, at
                    )
                edge[0, z] = total
            place_x = lax.broadcasted_iota(jnp.int32, (cells, LANES), 0) % rows
            for number in range(27):
                dx, dy = number // 3 % 3 - 1, number % 3 - 1
                weight = edge_windows(own_c[number], landed_c[0], landed_c[1], number)
                spread = jnp.zeros((cells, LANES), jnp.float32)
                for x in range(rows):
                    moved = turn(weight, 16 * (x + 1 + dx) + dy)
                    spread = jnp.where(place_x == x, moved, spread)
                for z in range(nz):
                    line = spread[z * rows : z * rows + 1]
                    for x in range(1, rows):
                        line = line + spread[z * rows + x : z * rows + x + 1]
                    wide_edge[number, z] = jnp.broadcast_to(line, (8, LANES))
            fill_padded(s)
        put_ghosts(s)
        apply_operator(s)
        if s + 1 < STEPS:
            send_rows(s + 1)
            send_edges(s + 1)

    local_gram(3)
    gram_over_gx(2)
    wait_gram(1)
    factor_block(1)
    apply_block(0)
    gram_over_gx(3)
    factor_block(2)
    apply_block(1)
    apply_block(2)
    for s in range(STEPS):
        for side in SIDES:
            row_copy(s, side).wait_send()
            if s > 0:
                edge_copy(s, side).wait_send()
    for side in SIDES:
        @pl.when(present[1 - side])
        def _():
            for slot in range(3):
                column_copy(side, slot).wait_send()
            coefficient_copy(side).wait_send()
    finish_gram(0)
    finish_gram(1)
    wait_gram(2)
    factor_block(3)
    apply_block(3)
    finish_gram(2)
    wait_gram(3)
    last_gram[...] = gram_block(last)
    finish_gram(3)


def finish_kernel(
    rhs, cells, high, low, first, last_gram, lower_inv, panels, upper, q_hbm, r_hbm,
    out, square, sem,
):
    total, last = BLOCKS * rhs, BLOCKS - 1
    store_first = pltpu.make_async_copy(first, q_hbm.at[pl.ds(0, last), :, :], sem.at[0])
    store_last = pltpu.make_async_copy(out, q_hbm.at[last], sem.at[1])
    store_square = pltpu.make_async_copy(square, r_hbm, sem.at[2])
    store_first.start()
    at = last * rhs
    panel, inverse, diagonal = factor_rows(last_gram[...], lower_inv[...], at, rhs, total)
    put_rows(inverse[:, 0:total], high[...], low[...], out, cells)
    store_last.start()
    pad = jnp.zeros((LANES - total, LANES), jnp.float32)
    lower = jnp.concatenate([panels[0:at, :], panel, pad], axis=0)
    diagonals = jnp.concatenate([upper[0:at, :], diagonal, pad], axis=0)
    square[...] = (jnp.transpose(lower) + diagonals)[0:total, 0:total]
    store_square.start()
    store_first.wait()
    store_last.wait()
    store_square.wait()


def local(nx, ny, right_sides, coefficients):
    rhs, nz, rows, columns = right_sides.shape
    cells = nz * rows
    total = BLOCKS * rhs
    size = rhs * cells
    f32, b16 = jnp.float32, jnp.bfloat16
    vmem = pl.BlockSpec(memory_space=pltpu.VMEM)
    hbm = pl.BlockSpec(memory_space=pltpu.HBM)
    shape = jax.ShapeDtypeStruct
    parts = pl.pallas_call(
        functools.partial(kernel, nx, ny, rhs, nz, rows, nx * ny * cells * columns),
        out_shape=(
            shape((total, cells * LANES), b16),
            shape((total, cells * LANES), b16),
            shape((BLOCKS - 1, size, columns), f32),
            shape((rhs, LANES), f32),
            shape((LANES, LANES), f32),
            shape((total, LANES), f32),
            shape((total, LANES), f32),
        ),
        in_specs=[hbm] * 2,
        out_specs=(vmem,) * 7,
        scratch_shapes=[
            pltpu.VMEM((size, columns), f32),
            pltpu.VMEM((27 * cells, columns), f32),
            pltpu.VMEM((27, cells, 8, LANES), f32),
            pltpu.VMEM((27, nz, 8, LANES), f32),
            pltpu.VMEM((STEPS, nz, rows, rhs, LANES), f32),
            pltpu.VMEM((STEPS, nz, rhs, LANES), f32),
            pltpu.VMEM((STEPS, 2, nz, rhs, LANES), f32),
            pltpu.VMEM((2, rhs, LANES), f32),
            pltpu.VMEM((2, 3, rhs, LANES), f32),
            pltpu.VMEM((2, cells, LANES), f32),
            pltpu.VMEM((2, cells, LANES), f32),
            pltpu.VMEM((STEPS, 2, 8, LANES), f32),
            pltpu.VMEM((STEPS, 2, 8, LANES), f32),
            pltpu.VMEM((nz, rows + 2, rhs, LANES), f32),
            pltpu.VMEM((nz, rhs, LANES), f32),
            pltpu.VMEM((cells, rhs, LANES), f32),
            pltpu.VMEM((27, cells, LANES), f32),
            pltpu.VMEM((2 * nx, total, LANES), f32),
            pltpu.VMEM((ny // 2, total, LANES), f32),
            pltpu.SemaphoreType.DMA((2,)),
            pltpu.SemaphoreType.DMA((STEPS, 8)),
            pltpu.SemaphoreType.DMA((STEPS, 8)),
            pltpu.SemaphoreType.DMA((2,)),
            pltpu.SemaphoreType.DMA((2,)),
            pltpu.SemaphoreType.DMA((len(GROUPS), 2 * nx)),
            pltpu.SemaphoreType.DMA((len(GROUPS), 2 * nx)),
            pltpu.SemaphoreType.DMA((len(GROUPS), ny // 2)),
            pltpu.SemaphoreType.DMA((len(GROUPS), ny // 2)),
        ],
        compiler_params=pltpu.CompilerParams(
            collective_id=0, has_side_effects=True, vmem_limit_bytes=32 * 1024 * 1024
        ),
    )(
        pltpu.with_memory_space_constraint(right_sides.reshape(size, columns), pltpu.HBM),
        pltpu.with_memory_space_constraint(coefficients.reshape(27 * cells, columns), pltpu.HBM),
    )
    solved, square = pl.pallas_call(
        functools.partial(finish_kernel, rhs, cells),
        out_shape=(shape((BLOCKS, size, columns), f32), shape((total, total), f32)),
        in_specs=[vmem] * 7,
        out_specs=(hbm, hbm),
        scratch_shapes=[
            pltpu.VMEM((size, columns), f32),
            pltpu.VMEM((total, total), f32),
            pltpu.SemaphoreType.DMA((3,)),
        ],
        compiler_params=pltpu.CompilerParams(vmem_limit_bytes=16 * 1024 * 1024),
    )(*parts)
    return solved.reshape(total, nz, rows, columns), square


def solution(mesh):
    placed = (P(None, None, "gx", "gy"), P(None, None, "gx", "gy"))
    return jax.shard_map(
        functools.partial(local, mesh.shape["gx"], mesh.shape["gy"]),
        mesh=mesh,
        in_specs=placed,
        out_specs=(P(None, None, "gx", "gy"), P()),
        check_vma=False,
    )
```
